32 devices in a mesh: docs: 8 (over z, y), rep: 4 (over x, core).
Axes of the slice: x: 2, y: 2, z: 4, core: 2. Of those that a mesh axis runs over, the one named last changes fastest.
Arguments:
- queries: bfloat16 [4096, 1024], P(('docs', 'rep')), may hold values from -6 to 6
- adapter: bfloat16 [1024, 1024], replicated, may hold values from -0.1875 to 0.1875
- doc_table: bfloat16 [8192, 1024], P(('docs', 'rep')), may hold values from -6 to 6
- routes: int32 [4096, 4], P(('docs', 'rep')), may hold values from 0 to 31, all different within a row; in each aligned block of 128 rows (0 to 127, 128 to 255, ...) at most 32 rows name the same one
- doc_rows: int32 [4096, 4, 16], P(('docs', 'rep')), may hold values from 0 to 255, as said below
- labels: int32 [4096, 4, 16], P(('docs', 'rep')), may hold values from 0 to 4
Outputs:
- losses: float32 [4096], P(('docs', 'rep'))
- query_grads: bfloat16 [4096, 1024], P(('docs', 'rep'))
- adapter_grad: bfloat16 [1024, 1024], P('docs')
The draws below stay inside these ranges and needn't reach their ends.
Inputs may be any that keep to these rules, and one draw needn't show every extreme that they name: `routes`: each query names 4 different owners; among the queries of one device no owner is named more than 32 times, and in every draw some owner is named exactly 32 times by some device's queries. `doc_rows`: the 16 rows of one query at one owner are distinct.
All inputs are finite; a program needn't handle non-finite values.
Results may differ from the reference program's by a relative error of at most 0.024.
Values may be sent and summed in bfloat16 or wider, within the bound.
A program may use at most 128 MiB of HBM per device.

```python
import math
import jax
import jax.numpy as jnp
import numpy as np
from jax import lax

D = 1024
QDEV = 128
DOC_DEV = 256
K = 4
M = 16
CAP = 32
QUERIES = 4096
NDOCS = 8192
DEVICES = 32


def draw_doc_rows(key, part):
    key_base, key_gaps = jax.random.split(key)
    start_rows = jax.random.randint(key_base, (QUERIES, K, 1), 0, DOC_DEV)
    gap_sizes = jax.random.randint(key_gaps, (QUERIES, K, M), 1, DOC_DEV // M + 1)
    offsets = jnp.cumsum(gap_sizes, axis=-1) - gap_sizes[:, :, :1]
    return ((start_rows + offsets) % DOC_DEV).astype(jnp.int32)


def place_ends(array, key, least, largest):
    extent = array.shape
    place = [jax.random.randint(jax.random.fold_in(key, axis), (), 0, extent[axis]) for axis in range(len(extent))]
    array = array.at[tuple(place)].set(least)
    longest = extent.index(max(extent))
    place[longest] = (place[longest] + 1) % extent[longest]
    return array.at[tuple(place)].set(largest)


def level_of(key, extent, shards, low, top_value):
    factor_of = 1.0
    for dim, shards_of in shards:
        steps = jax.random.uniform(jax.random.fold_in(jax.random.fold_in(key, 6), dim), (shards_of,), jnp.float32, low / len(shards), top_value / len(shards))
        factor_of = factor_of * jnp.repeat(jnp.exp(steps), extent[dim] // shards_of).reshape((-1,) + (1,) * (len(extent) - 1 - dim))
    return factor_of


def routed_block(own_key, own, number, rows, count, top, most, slope):
    sequence = jax.random.permutation(own_key, count)
    heavy_load, common = portions_of(count, rows * top, most, slope, True), portions_of(count, rows * top, most, slope, False)
    places = jnp.arange(count)

    def named(lengths, rotation):
        used = int((lengths > 0).sum())
        fixed = max(1, used // 4)
        shifted = fixed + (places - fixed + rotation * (used - fixed)) % max(1, count - fixed)
        return jnp.zeros((count,), jnp.int32).at[sequence[jnp.where(places < fixed, places, shifted)]].set(jnp.asarray(lengths, jnp.int32))

    lengths = jnp.where(number % 4 == 0, named(heavy_load, number // 4), named(common, number - number // 4 - 1))
    mixed = jax.random.permutation(jax.random.fold_in(own, 3), count)
    giver, sink = mixed[0:count // 2 * 2:2], mixed[1:count // 2 * 2:2]
    room = jnp.minimum(lengths[giver] - 1, most - lengths[sink]) // 2
    room = jnp.where((giver == sequence[0]) | (sink == sequence[0]) | (lengths[sink] == 0), 0, jnp.maximum(room, 0))
    shifted = jax.random.randint(jax.random.fold_in(own, 4), (count // 2,), 0, 1 << 20) % (room + 1)
    lengths = lengths.at[giver].add(-shifted).at[sink].add(shifted)
    members = jnp.searchsorted(jnp.cumsum(lengths), jnp.arange(rows * top), side="right").astype(jnp.int32)
    table = members.reshape(top, rows).T
    table = table[jax.random.permutation(jax.random.fold_in(own, 1), rows)]
    rotation = jax.random.randint(jax.random.fold_in(own, 2), (rows, 1), 0, top)
    return jnp.take_along_axis(table, (jnp.arange(top)[None, :] + rotation) % top, axis=1)


def portions_of(count, total, limit, slope, full):
    portions = [(1 << 20) // math.isqrt(rank ** slope) + 1 for rank in range(1, count + 1)]
    largest = limit if full else min(limit, max(-(-total // count), total * portions[0] // sum(portions)))
    least = 1 if total - largest >= count - 1 else 0
    counts, rest = [largest] + [least] * (count - 1), total - largest - least * (count - 1)
    while rest > 0:
        movable = [i for i in range(1, count) if counts[i] < largest] or [i for i in range(1, count) if counts[i] < limit]
        pool, budget = sum([portions[i] for i in movable]), rest
        for i in movable:
            more = min(limit - counts[i], max(1, budget * portions[i] // pool), rest)
            counts[i] = counts[i] + more
            rest = rest - more
    return np.array(counts)


def centred(rng, shape, scale, most, cuts=(), kind=jnp.bfloat16):
    result = scale * jax.random.normal(rng, shape, jnp.float32)
    if cuts:
        result = result * level_of(rng, shape, cuts, -0.22, 0.18)
    return jnp.clip(result, -most, most).astype(kind)


def setup_inputs(seed: int = 0) -> dict:
    streams_of = jax.random.split(jax.random.key(seed), 7)
    queries = centred(streams_of[0], (QUERIES, D), 1.0, 6.0, ((0, 32),))
    adapter = centred(streams_of[1], (D, D), D ** -0.5, 0.1875)
    doc_table = centred(streams_of[2], (NDOCS, D), 1.0, 6.0, ((0, 32),))
    routes_keys = jax.random.split(jax.random.fold_in(streams_of[3], 1), QUERIES // QDEV)
    routes_turns = jax.random.permutation(jax.random.fold_in(streams_of[3], 3), QUERIES // QDEV)
    routes = jax.vmap(lambda own, number: routed_block(jax.random.fold_in(streams_of[3], 2), own, number, QDEV, DEVICES, K, CAP, 1))(routes_keys, routes_turns).reshape((QUERIES, K))
    doc_rows = draw_doc_rows(jax.random.fold_in(streams_of[6], 71), 0)
    labels = place_ends(jax.random.randint(streams_of[5], (QUERIES, K, M), 0, 5), jax.random.fold_in(streams_of[5], 1), 0, 4).astype(jnp.int32)
    return dict(queries=queries, adapter=adapter, doc_table=doc_table, routes=routes, doc_rows=doc_rows, labels=labels)


EPSILON = 1e-06
LOSS_SCALE = 128.0

def unit_rows(rows):
    widened = rows.astype(jnp.float32)
    return (widened / jnp.sqrt(lax.optimization_barrier(jnp.mean(widened * widened, axis=-1, keepdims=True)) + EPSILON)).astype(jnp.bfloat16)

def reference(queries, adapter, doc_table, routes, doc_rows, labels):
    score_scale = 2.0 / math.sqrt(D)
    adapted = jnp.dot(queries, adapter, preferred_element_type=jnp.float32)
    radius = jnp.sqrt(lax.optimization_barrier(jnp.mean(adapted * adapted, axis=-1, keepdims=True)) + EPSILON)
    unit_exact = adapted / radius
    unit_query = unit_exact.astype(jnp.bfloat16)
    blocks = QUERIES // QDEV

    def one_block(pieces):
        unit_part, route_part, row_part, label_part = pieces
        cand_rows = route_part[:, :, None] * DOC_DEV + row_part
        candidates = unit_rows(doc_table[cand_rows]).astype(jnp.float32)
        scores = jnp.einsum('qd,qkmd->qkm', unit_part.astype(jnp.float32), candidates) * score_scale
        raised = jnp.exp(scores)
        norm_total = lax.optimization_barrier(jnp.sum(raised, axis=(1, 2)))
        label_weight = jnp.exp(label_part.astype(jnp.float32))
        target = label_weight / lax.optimization_barrier(jnp.sum(label_weight, axis=(1, 2), keepdims=True))
        losses = jnp.log(norm_total) - lax.optimization_barrier(jnp.sum(target * scores, axis=(1, 2)))
        weights = (LOSS_SCALE * (raised / norm_total[:, None, None] - target)).astype(jnp.bfloat16)
        pull_rows = (jnp.einsum('qkm,qkmd->qkd', weights.astype(jnp.float32), candidates) * score_scale).astype(jnp.bfloat16)
        pull_total = lax.optimization_barrier(jnp.sum(pull_rows.astype(jnp.float32), axis=1))
        return (losses, pull_total)
    losses, pull_total = lax.map(one_block, (unit_query.reshape(blocks, QDEV, D), routes.reshape(blocks, QDEV, K), doc_rows.reshape(blocks, QDEV, K, M), labels.reshape(blocks, QDEV, K, M)))
    losses = losses.reshape(QUERIES)
    pull_total = pull_total.reshape(QUERIES, D)
    projection = lax.optimization_barrier(jnp.mean(unit_exact * pull_total, axis=-1, keepdims=True))
    adapted_grad = ((pull_total - unit_exact * projection) / radius).astype(jnp.bfloat16)
    query_grads = lax.dot_general(adapted_grad, adapter, (((1,), (1,)), ((), ())), preferred_element_type=jnp.float32).astype(jnp.bfloat16)
    summed = lax.dot_general(queries, adapted_grad, (((0,), (0,)), ((), ())), preferred_element_type=jnp.float32)
    adapter_grad = (summed * (1.0 / math.sqrt(QUERIES))).astype(jnp.bfloat16)
    return (losses, query_grads, adapter_grad)
```

```python
import functools
import math

import jax
import jax.numpy as jnp
from jax import lax
from jax.experimental import pallas as pl
from jax.experimental.pallas import tpu as pltpu
from jax.sharding import PartitionSpec as P

EPSILON = 1e-06
LOSS_SCALE = 128.0
MESH = pl.DeviceIdType.MESH
GATHER_LIMIT = 8 * 1024 * 1024


def unit_rows(rows):
    widened = rows.astype(jnp.float32)
    return (
        widened / jnp.sqrt(jnp.mean(widened * widened, axis=-1, keepdims=True) + EPSILON)
    ).astype(jnp.bfloat16)


def routed_on_device(queries, adapter, doc_table, routes, doc_rows, labels):
    doc_groups = lax.axis_size("docs")
    rep_groups = lax.axis_size("rep")
    devices = doc_groups * rep_groups
    query_rows, feature_width = queries.shape
    fanout = routes.shape[1]
    per_owner = doc_rows.shape[2]
    doc_count = doc_table.shape[0]
    capacity = max(2, 2 * query_rows * fanout // devices)
    slots_all = devices * capacity
    score_scale = 2.0 / math.sqrt(feature_width)
    adapted = jnp.dot(queries, adapter, preferred_element_type=jnp.float32)
    radius = jnp.sqrt(jnp.mean(adapted * adapted, axis=-1, keepdims=True) + EPSILON)
    unit_exact = adapted / radius
    unit_query = unit_exact.astype(jnp.bfloat16)
    owner_hits = (routes[:, :, None] == jnp.arange(devices, dtype=jnp.int32)[None, None, :]).astype(
        jnp.int32
    )
    per_query = jnp.sum(owner_hits, axis=1)
    row_index = jnp.arange(query_rows, dtype=jnp.int32)
    lower_table = (row_index[:, None] > row_index[None, :]).astype(jnp.float32)
    earlier = jnp.dot(
        lower_table, per_query.astype(jnp.float32), precision=lax.Precision.HIGHEST
    ).astype(jnp.int32)
    slot_index = jnp.sum(earlier[:, None, :] * owner_hits, axis=-1)
    placed = routes * capacity + slot_index
    target_slot = placed.reshape(-1)
    repeated = jnp.broadcast_to(
        unit_query[:, None, :], (query_rows, fanout, feature_width)
    ).reshape(-1, feature_width)
    outgoing = jnp.zeros((slots_all, feature_width), jnp.bfloat16).at[target_slot].set(repeated)
    outgoing_ids = (
        jnp.zeros((slots_all, per_owner), jnp.int32)
        .at[target_slot]
        .set(doc_rows.reshape(-1, per_owner))
    )
    outgoing = outgoing.reshape(doc_groups, rep_groups, capacity, feature_width)
    outgoing_ids = outgoing_ids.reshape(doc_groups, rep_groups, capacity, per_owner)
    arrived, arrived_ids = (
        lax.all_to_all(
            lax.all_to_all(outgoing, "docs", split_axis=0, concat_axis=0, tiled=True),
            "rep",
            split_axis=1,
            concat_axis=1,
            tiled=True,
        ),
        lax.all_to_all(
            lax.all_to_all(outgoing_ids, "docs", split_axis=0, concat_axis=0, tiled=True),
            "rep",
            split_axis=1,
            concat_axis=1,
            tiled=True,
        ),
    )
    arrived = arrived.reshape(slots_all, feature_width)
    arrived_ids = arrived_ids.reshape(slots_all, per_owner)
    doc_unit = unit_rows(doc_table)
    block_scores = lax.dot_general(
        arrived, doc_unit, (((1,), (1,)), ((), ())), preferred_element_type=jnp.float32
    )
    scores_out = jnp.take_along_axis(block_scores, arrived_ids, axis=1) * score_scale
    returned = lax.all_to_all(
        lax.all_to_all(
            scores_out.reshape(doc_groups, rep_groups, capacity, per_owner).astype(jnp.bfloat16),
            "docs",
            split_axis=0,
            concat_axis=0,
            tiled=True,
        ),
        "rep",
        split_axis=1,
        concat_axis=1,
        tiled=True,
    ).astype(jnp.float32)
    scores = returned.reshape(slots_all, per_owner)[placed]
    raised = jnp.exp(scores)
    norm_total = jnp.sum(raised, axis=(1, 2))
    label_weight = jnp.exp(labels.astype(jnp.float32))
    target = label_weight / jnp.sum(label_weight, axis=(1, 2), keepdims=True)
    losses = jnp.log(norm_total) - jnp.sum(target * scores, axis=(1, 2))
    weights = (LOSS_SCALE * (raised / norm_total[:, None, None] - target)).astype(jnp.bfloat16)
    weight_slots = (
        jnp.zeros((slots_all, per_owner), jnp.bfloat16)
        .at[target_slot]
        .set(weights.reshape(-1, per_owner))
    )
    weights_in = lax.all_to_all(
        lax.all_to_all(
            weight_slots.reshape(doc_groups, rep_groups, capacity, per_owner),
            "docs",
            split_axis=0,
            concat_axis=0,
            tiled=True,
        ),
        "rep",
        split_axis=1,
        concat_axis=1,
        tiled=True,
    )
    weights_in = weights_in.reshape(slots_all, per_owner)
    spread = (
        jnp.zeros((slots_all, doc_count), jnp.bfloat16)
        .at[jnp.arange(slots_all)[:, None], arrived_ids]
        .set(weights_in)
    )
    pull_out = (jnp.dot(spread, doc_unit, preferred_element_type=jnp.float32) * score_scale).astype(
        jnp.bfloat16
    )
    pull_out = pull_out.reshape(doc_groups, rep_groups, capacity, feature_width)
    pull_back = lax.all_to_all(
        lax.all_to_all(pull_out, "docs", split_axis=0, concat_axis=0, tiled=True),
        "rep",
        split_axis=1,
        concat_axis=1,
        tiled=True,
    )
    pull_rows = pull_back.reshape(slots_all, feature_width)[placed]
    pull_total = jnp.sum(pull_rows.astype(jnp.float32), axis=1)
    projection = jnp.mean(unit_exact * pull_total, axis=-1, keepdims=True)
    adapted_grad = ((pull_total - unit_exact * projection) / radius).astype(jnp.bfloat16)
    query_grads = lax.dot_general(
        adapted_grad, adapter, (((1,), (1,)), ((), ())), preferred_element_type=jnp.float32
    ).astype(jnp.bfloat16)
    inverse_root = 1.0 / math.sqrt(query_rows * devices)
    local_terms = lax.dot_general(
        queries, adapted_grad, (((0,), (0,)), ((), ())), preferred_element_type=jnp.float32
    )
    group_terms = lax.psum(local_terms.astype(jnp.bfloat16), "rep").astype(jnp.float32)
    summed = lax.psum_scatter(group_terms, "docs", scatter_dimension=0, tiled=True)
    adapter_grad = (summed * inverse_root).astype(jnp.bfloat16)
    return (losses, query_grads, adapter_grad)


def dot_nt(a, b):
    return lax.dot_general(a, b, (((1,), (1,)), ((), ())), preferred_element_type=jnp.float32)


def dot_tn(a, b):
    return lax.dot_general(a, b, (((0,), (0,)), ((), ())), preferred_element_type=jnp.float32)


def ring_group(position, groups):
    column = position // (groups // 2)
    along = position + column * (groups - 1 - 2 * position)
    return 2 * along + column


def gathered_kernel(
    groups, reps, fanout, per_owner, inverse_root,
    queries_ref, adapter_ref, doc_ref, meta_ref,
    loss_ref, query_grad_ref, adapter_grad_ref,
    docs_all, unit_all, raw_all, meta_all, unit_exact_ref, radius_ref,
    raised_all, target_all, score_ref, label_sum, stats, stats_in, weight_ref,
    pull_out, pull_in, grad_cols, grad_in, terms_out, terms_in, final_cols,
    ring_send, ring_recv, rep_send, rep_recv, small_send, small_recv,
    terms_send, terms_recv,
):
    docs_at = lax.axis_index("docs")
    rep_at = lax.axis_index("rep")
    rows, width = queries_ref.shape
    doc_count = doc_ref.shape[0]
    half = doc_count // 2
    others = reps - 1
    candidates = fanout * per_owner
    score_scale = 2.0 / math.sqrt(width)

    def rep_peer(step):
        return lax.rem(rep_at + step, reps)

    along, column = docs_at // 2, docs_at % 2
    place = along + column * (groups - 1 - 2 * along)
    right = ring_group(lax.rem(place + 1, groups), groups)
    left = ring_group(lax.rem(place + groups - 1, groups), groups)

    barrier = pltpu.get_barrier_semaphore()
    for step in range(1, reps):
        pl.semaphore_signal(
            barrier, inc=1, device_id=(docs_at, rep_peer(step)), device_id_type=MESH
        )
    for step in range(1, groups):
        pl.semaphore_signal(
            barrier, inc=1, device_id=(lax.rem(docs_at + step, groups), rep_at), device_id_type=MESH
        )
    docs_all[0] = unit_rows(doc_ref[...])
    pl.semaphore_wait(barrier, others + groups - 1)

    def ring_copy(way, index):
        hop = index // 2
        if way == 0:
            part, source, landing, device = index % 2, hop, hop + 1, right
        else:
            part, source, landing, device = (
                1 - index % 2, (groups - hop) % groups, groups - hop - 1, left
            )
        return pltpu.make_async_remote_copy(
            src_ref=docs_all.at[source, pl.ds(part * half, half)],
            dst_ref=docs_all.at[landing, pl.ds(part * half, half)],
            send_sem=ring_send.at[way, index],
            recv_sem=ring_recv.at[way, index],
            device_id=(device, rep_at),
            device_id_type=MESH,
        )

    ring_steps = groups - 1
    for index in range(2):
        for way in range(2):
            ring_copy(way, index).start()

    def rep_copy(kind, at, source, landing):
        return pltpu.make_async_remote_copy(
            src_ref=source,
            dst_ref=landing,
            send_sem=rep_send.at[kind, at],
            recv_sem=rep_recv.at[kind, at],
            device_id=(docs_at, rep_peer(at + 1)),
            device_id_type=MESH,
        )

    meta_copies = [rep_copy(0, at, meta_ref, meta_all.at[at]) for at in range(others)]
    for copy in meta_copies:
        copy.start()
    adapted = jnp.dot(queries_ref[...], adapter_ref[...], preferred_element_type=jnp.float32)
    radius = jnp.sqrt(jnp.mean(adapted * adapted, axis=-1, keepdims=True) + EPSILON)
    unit_exact = adapted / radius
    unit_exact_ref[...] = unit_exact
    radius_ref[...] = radius
    unit_all[others] = unit_exact.astype(jnp.bfloat16)
    unit_copies = [rep_copy(1, at, unit_all.at[others], unit_all.at[at]) for at in range(others)]
    for copy in unit_copies:
        copy.start()
    raw_copies = [rep_copy(2, at, queries_ref, raw_all.at[at]) for at in range(others)]
    for copy in raw_copies:
        copy.start()
    raw_all[others] = queries_ref[...]
    meta_all[others] = meta_ref[...]
    stats[...] = jnp.zeros_like(stats)

    tile = 64
    tiles = doc_count // tile

    def label_mask(slot):
        owner = ring_group(lax.rem(place + groups - slot, groups), groups) * reps + rep_at

        def step(index, carry):
            at = index // tiles
            first = pl.multiple_of((index % tiles) * tile, tile)
            lanes = pl.ds(pl.multiple_of(at * rows, rows), rows)
            owners = meta_all[at, 2 * candidates : 2 * candidates + 8, :]
            ids = jnp.full((per_owner, rows), -1, jnp.int32)
            marks = jnp.zeros((per_owner, rows), jnp.int32)
            for k in range(fanout):
                named = owners[k : k + 1, :] == owner
                ids = jnp.where(named, meta_all[at, k * per_owner : (k + 1) * per_owner, :], ids)
                low = candidates + k * per_owner
                marks = jnp.where(named, meta_all[at, low : low + per_owner, :] + 1, marks)
            marks = marks.astype(jnp.float32)
            here = lax.broadcasted_iota(jnp.int32, (tile, rows), 0) + first
            found = jnp.zeros((tile, rows), jnp.float32)
            for m in range(per_owner):
                found = jnp.where(here == ids[m : m + 1, :], marks[m : m + 1, :], found)
            target_all[slot, pl.ds(first, tile), lanes] = found
            return carry

        lax.fori_loop(0, reps * tiles, step, 0)

    def score(slot):
        score_ref[...] = (
            dot_nt(docs_all[slot], unit_all[...].reshape(reps * rows, width)) * score_scale
        )
        for at in range(reps):
            lanes = pl.ds(at * rows, rows)

            def step(index, totals):
                span = pl.ds(pl.multiple_of(index * tile, tile), tile)
                marks = target_all[slot, span, lanes]
                scores = score_ref[span, lanes]
                held = marks > 0.5
                raised = jnp.where(held, jnp.exp(scores), 0.0)
                target = jnp.where(held, jnp.exp(marks - 1.0), 0.0) * label_sum[at, 0:1, :]
                raised_all[slot, span, lanes] = raised
                target_all[slot, span, lanes] = target * LOSS_SCALE
                return (
                    totals[0] + jnp.sum(raised, axis=0, keepdims=True),
                    totals[1] + jnp.sum(target * scores, axis=0, keepdims=True),
                )

            zero = jnp.zeros((1, rows), jnp.float32)
            norm, dotted = lax.fori_loop(0, tiles, step, (zero, zero))
            stats[at, 0:1, :] += norm
            stats[at, 1:2, :] += dotted

    for index in range(ring_steps):
        for way in range(2):
            ring_copy(way, index).wait_recv()
            if index + 2 < ring_steps:
                ring_copy(way, index + 2).start()
        if index == 0:
            for copy in meta_copies:
                copy.wait_recv()
            for at in range(reps):
                raised_labels = jnp.exp(
                    meta_all[at, candidates : 2 * candidates, :].astype(jnp.float32)
                )
                label_sum[at, 0:1, :] = 1.0 / jnp.sum(raised_labels, axis=0, keepdims=True)
            for slot in range(4):
                label_mask(slot)
        elif index == 1:
            for slot in range(4, groups):
                label_mask(slot)
        elif index == 2:
            for copy in unit_copies:
                copy.wait_recv()
            score(0)
            score(1)
            score(groups - 1)
        elif index % 2 == 0:
            score(index // 2)
            score(groups - index // 2)
    score(groups // 2)

    def small_copy(kind, at, peer, source, landing):
        return pltpu.make_async_remote_copy(
            src_ref=source,
            dst_ref=landing,
            send_sem=small_send.at[kind, at],
            recv_sem=small_recv.at[kind, at],
            device_id=(docs_at, peer),
            device_id_type=MESH,
        )

    stat_copies = [
        small_copy(0, at, rep_peer(at + 1), stats, stats_in.at[at]) for at in range(others)
    ]
    for copy in stat_copies:
        copy.start()
    for copy in stat_copies:
        copy.wait_recv()
    norms = []
    for at in range(reps):
        total = stats[at]
        for origin in range(others):
            total = total + stats_in[origin, (at - origin - 1) % reps]
        norms.append(total)
    loss_ref[...] = jnp.log(norms[others][0:1, :]) - norms[others][1:2, :]

    pull_copies = [
        small_copy(1, at, rep_peer(reps - at - 1), pull_out.at[at], pull_in.at[at])
        for at in range(others)
    ]
    all_docs = docs_all[...].reshape(groups * doc_count, width)
    own_pull = None
    for pair in range(reps // 2):
        for at in (2 * pair, 2 * pair + 1):
            share = LOSS_SCALE / norms[at][0:1, :]
            lanes = pl.ds(at * rows, rows)

            def weigh(slot, carry):
                weight_ref[slot, :, lanes] = (
                    raised_all[slot, :, lanes] * share - target_all[slot, :, lanes]
                ).astype(jnp.bfloat16)
                return carry

            lax.fori_loop(0, groups, weigh, 0)
        lanes = pl.ds(2 * pair * rows, 2 * rows)
        pulled = (
            dot_tn(weight_ref[:, :, lanes].reshape(groups * doc_count, 2 * rows), all_docs)
            * score_scale
        )
        for at in (2 * pair, 2 * pair + 1):
            low = (at - 2 * pair) * rows
            if at < others:
                pull_out[at] = pulled[low : low + rows].astype(jnp.bfloat16)
                pull_copies[at].start()
            else:
                own_pull = pulled[low : low + rows]
    pull_total = own_pull
    for at in range(others):
        pull_copies[at].wait_recv()
        pull_total = pull_total + pull_in[at].astype(jnp.float32)
    unit = unit_exact_ref[...]
    projection = jnp.mean(unit * pull_total, axis=-1, keepdims=True)
    adapted_grad = ((pull_total - unit * projection) / radius_ref[...]).astype(jnp.bfloat16)
    block = width // reps
    for at in range(reps):
        grad_cols[at] = adapted_grad[:, at * block : (at + 1) * block]
    grad_copies = [
        small_copy(2, at, rep_peer(at + 1), grad_cols.at[rep_peer(at + 1)], grad_in.at[at])
        for at in range(others)
    ]
    for copy in grad_copies:
        copy.start()
    grad_in[others] = grad_cols[rep_at]
    query_grad_ref[...] = dot_nt(adapted_grad, adapter_ref[...]).astype(jnp.bfloat16)
    for at in range(others):
        raw_copies[at].wait_recv()
        grad_copies[at].wait_recv()
    group_terms = dot_tn(
        raw_all[...].reshape(reps * rows, width), grad_in[...].reshape(reps * rows, block)
    )
    out_rows = width // groups
    terms_out[...] = group_terms.astype(jnp.bfloat16).reshape(groups, out_rows, block)
    term_copies = []
    for step in range(1, groups):
        peer = lax.rem(docs_at + step, groups)
        copy = pltpu.make_async_remote_copy(
            src_ref=terms_out.at[peer],
            dst_ref=terms_in.at[step - 1],
            send_sem=terms_send.at[step - 1],
            recv_sem=terms_recv.at[step - 1],
            device_id=(peer, rep_at),
            device_id_type=MESH,
        )
        copy.start()
        term_copies.append(copy)
    summed = terms_out[docs_at].astype(jnp.float32)
    for step in range(groups - 1):
        term_copies[step].wait_recv()
        summed = summed + terms_in[step].astype(jnp.float32)
    final_cols[rep_at] = (summed * inverse_root).astype(jnp.bfloat16)
    final_copies = [
        small_copy(3, at, rep_peer(at + 1), final_cols.at[rep_at], final_cols.at[rep_at])
        for at in range(others)
    ]
    for copy in final_copies:
        copy.start()
    for copy in final_copies:
        copy.wait_recv()
    for at in range(reps):
        adapter_grad_ref[:, at * block : (at + 1) * block] = final_cols[at]

    for index in range(ring_steps):
        for way in range(2):
            ring_copy(way, index).wait_send()
    for copy in (
        meta_copies + unit_copies + raw_copies + stat_copies + pull_copies
        + grad_copies + term_copies + final_copies
    ):
        copy.wait_send()


def gathered_on_device(queries, adapter, doc_table, routes, doc_rows, labels):
    groups = lax.axis_size("docs")
    reps = lax.axis_size("rep")
    rows, width = queries.shape
    fanout = routes.shape[1]
    per_owner = doc_rows.shape[2]
    doc_count = doc_table.shape[0]
    candidates = fanout * per_owner
    block = width // reps
    out_rows = width // groups
    others = reps - 1
    meta = jnp.concatenate(
        [
            doc_rows.reshape(rows, candidates),
            labels.reshape(rows, candidates),
            routes,
            jnp.zeros((rows, 8 - fanout), jnp.int32),
        ],
        axis=1,
    ).T
    meta_rows = meta.shape[0]
    bf16, f32 = jnp.bfloat16, jnp.float32
    vmem = pltpu.VMEM
    dma = pltpu.SemaphoreType.DMA
    losses, query_grads, adapter_grad = pl.pallas_call(
        functools.partial(
            gathered_kernel, groups, reps, fanout, per_owner,
            1.0 / math.sqrt(rows * groups * reps),
        ),
        out_shape=(
            jax.ShapeDtypeStruct((1, rows), f32),
            jax.ShapeDtypeStruct((rows, width), bf16),
            jax.ShapeDtypeStruct((out_rows, width), bf16),
        ),
        in_specs=[pl.BlockSpec(memory_space=vmem)] * 4,
        out_specs=[pl.BlockSpec(memory_space=vmem)] * 3,
        scratch_shapes=[
            vmem((groups, doc_count, width), bf16),
            vmem((reps, rows, width), bf16),
            vmem((reps, rows, width), bf16),
            vmem((reps, meta_rows, rows), jnp.int32),
            vmem((rows, width), f32),
            vmem((rows, 1), f32),
            vmem((groups, doc_count, reps * rows), f32),
            vmem((groups, doc_count, reps * rows), f32),
            vmem((doc_count, reps * rows), f32),
            vmem((reps, 8, rows), f32),
            vmem((reps, 8, rows), f32),
            vmem((others, reps, 8, rows), f32),
            vmem((groups, doc_count, reps * rows), bf16),
            vmem((others, rows, width), bf16),
            vmem((others, rows, width), bf16),
            vmem((reps, rows, block), bf16),
            vmem((reps, rows, block), bf16),
            vmem((groups, out_rows, block), bf16),
            vmem((groups - 1, out_rows, block), bf16),
            vmem((reps, out_rows, block), bf16),
            dma((2, groups - 1)),
            dma((2, groups - 1)),
            dma((3, others)),
            dma((3, others)),
            dma((4, others)),
            dma((4, others)),
            dma((groups - 1,)),
            dma((groups - 1,)),
        ],
        compiler_params=pltpu.CompilerParams(
            collective_id=0, has_side_effects=True, vmem_limit_bytes=48 * 1024 * 1024
        ),
    )(queries, adapter, doc_table, meta)
    return (losses.reshape(rows), query_grads, adapter_grad)


def on_device(queries, adapter, doc_table, routes, doc_rows, labels):
    gathered_bytes = lax.axis_size("docs") * doc_table.size * doc_table.dtype.itemsize
    if gathered_bytes <= GATHER_LIMIT and lax.axis_size("rep") % 2 == 0:
        return gathered_on_device(queries, adapter, doc_table, routes, doc_rows, labels)
    return routed_on_device(queries, adapter, doc_table, routes, doc_rows, labels)


def solution(mesh):
    placed = (
        P(("docs", "rep"), None),
        P(),
        P(("docs", "rep"), None),
        P(("docs", "rep"), None),
        P(("docs", "rep"), None, None),
        P(("docs", "rep"), None, None),
    )
    return jax.shard_map(
        on_device,
        mesh=mesh,
        in_specs=placed,
        out_specs=(P(("docs", "rep")), P(("docs", "rep"), None), P("docs", None)),
        check_vma=False,
    )
```

```python
import functools
import math

import jax
import jax.numpy as jnp
from jax import lax
from jax.experimental import pallas as pl
from jax.experimental.pallas import tpu as pltpu
from jax.sharding import PartitionSpec as P

EPSILON = 1e-06
LOSS_SCALE = 128.0
MESH = pl.DeviceIdType.MESH
GATHER_LIMIT = 8 * 1024 * 1024


def unit_rows(rows):
    widened = rows.astype(jnp.float32)
    return (
        widened / jnp.sqrt(jnp.mean(widened * widened, axis=-1, keepdims=True) + EPSILON)
    ).astype(jnp.bfloat16)


def routed_on_device(queries, adapter, doc_table, routes, doc_rows, labels):
    doc_groups = lax.axis_size("docs")
    rep_groups = lax.axis_size("rep")
    devices = doc_groups * rep_groups
    query_rows, feature_width = queries.shape
    fanout = routes.shape[1]
    per_owner = doc_rows.shape[2]
    doc_count = doc_table.shape[0]
    capacity = max(2, 2 * query_rows * fanout // devices)
    slots_all = devices * capacity
    score_scale = 2.0 / math.sqrt(feature_width)
    adapted = jnp.dot(queries, adapter, preferred_element_type=jnp.float32)
    radius = jnp.sqrt(jnp.mean(adapted * adapted, axis=-1, keepdims=True) + EPSILON)
    unit_exact = adapted / radius
    unit_query = unit_exact.astype(jnp.bfloat16)
    owner_hits = (routes[:, :, None] == jnp.arange(devices, dtype=jnp.int32)[None, None, :]).astype(
        jnp.int32
    )
    per_query = jnp.sum(owner_hits, axis=1)
    row_index = jnp.arange(query_rows, dtype=jnp.int32)
    lower_table = (row_index[:, None] > row_index[None, :]).astype(jnp.float32)
    earlier = jnp.dot(
        lower_table, per_query.astype(jnp.float32), precision=lax.Precision.HIGHEST
    ).astype(jnp.int32)
    slot_index = jnp.sum(earlier[:, None, :] * owner_hits, axis=-1)
    placed = routes * capacity + slot_index
    target_slot = placed.reshape(-1)
    repeated = jnp.broadcast_to(
        unit_query[:, None, :], (query_rows, fanout, feature_width)
    ).reshape(-1, feature_width)
    outgoing = jnp.zeros((slots_all, feature_width), jnp.bfloat16).at[target_slot].set(repeated)
    outgoing_ids = (
        jnp.zeros((slots_all, per_owner), jnp.int32)
        .at[target_slot]
        .set(doc_rows.reshape(-1, per_owner))
    )
    outgoing = outgoing.reshape(doc_groups, rep_groups, capacity, feature_width)
    outgoing_ids = outgoing_ids.reshape(doc_groups, rep_groups, capacity, per_owner)
    arrived, arrived_ids = (
        lax.all_to_all(
            lax.all_to_all(outgoing, "docs", split_axis=0, concat_axis=0, tiled=True),
            "rep",
            split_axis=1,
            concat_axis=1,
            tiled=True,
        ),
        lax.all_to_all(
            lax.all_to_all(outgoing_ids, "docs", split_axis=0, concat_axis=0, tiled=True),
            "rep",
            split_axis=1,
            concat_axis=1,
            tiled=True,
        ),
    )
    arrived = arrived.reshape(slots_all, feature_width)
    arrived_ids = arrived_ids.reshape(slots_all, per_owner)
    doc_unit = unit_rows(doc_table)
    block_scores = lax.dot_general(
        arrived, doc_unit, (((1,), (1,)), ((), ())), preferred_element_type=jnp.float32
    )
    scores_out = jnp.take_along_axis(block_scores, arrived_ids, axis=1) * score_scale
    returned = lax.all_to_all(
        lax.all_to_all(
            scores_out.reshape(doc_groups, rep_groups, capacity, per_owner).astype(jnp.bfloat16),
            "docs",
            split_axis=0,
            concat_axis=0,
            tiled=True,
        ),
        "rep",
        split_axis=1,
        concat_axis=1,
        tiled=True,
    ).astype(jnp.float32)
    scores = returned.reshape(slots_all, per_owner)[placed]
    raised = jnp.exp(scores)
    norm_total = jnp.sum(raised, axis=(1, 2))
    label_weight = jnp.exp(labels.astype(jnp.float32))
    target = label_weight / jnp.sum(label_weight, axis=(1, 2), keepdims=True)
    losses = jnp.log(norm_total) - jnp.sum(target * scores, axis=(1, 2))
    weights = (LOSS_SCALE * (raised / norm_total[:, None, None] - target)).astype(jnp.bfloat16)
    weight_slots = (
        jnp.zeros((slots_all, per_owner), jnp.bfloat16)
        .at[target_slot]
        .set(weights.reshape(-1, per_owner))
    )
    weights_in = lax.all_to_all(
        lax.all_to_all(
            weight_slots.reshape(doc_groups, rep_groups, capacity, per_owner),
            "docs",
            split_axis=0,
            concat_axis=0,
            tiled=True,
        ),
        "rep",
        split_axis=1,
        concat_axis=1,
        tiled=True,
    )
    weights_in = weights_in.reshape(slots_all, per_owner)
    spread = (
        jnp.zeros((slots_all, doc_count), jnp.bfloat16)
        .at[jnp.arange(slots_all)[:, None], arrived_ids]
        .set(weights_in)
    )
    pull_out = (jnp.dot(spread, doc_unit, preferred_element_type=jnp.float32) * score_scale).astype(
        jnp.bfloat16
    )
    pull_out = pull_out.reshape(doc_groups, rep_groups, capacity, feature_width)
    pull_back = lax.all_to_all(
        lax.all_to_all(pull_out, "docs", split_axis=0, concat_axis=0, tiled=True),
        "rep",
        split_axis=1,
        concat_axis=1,
        tiled=True,
    )
    pull_rows = pull_back.reshape(slots_all, feature_width)[placed]
    pull_total = jnp.sum(pull_rows.astype(jnp.float32), axis=1)
    projection = jnp.mean(unit_exact * pull_total, axis=-1, keepdims=True)
    adapted_grad = ((pull_total - unit_exact * projection) / radius).astype(jnp.bfloat16)
    query_grads = lax.dot_general(
        adapted_grad, adapter, (((1,), (1,)), ((), ())), preferred_element_type=jnp.float32
    ).astype(jnp.bfloat16)
    inverse_root = 1.0 / math.sqrt(query_rows * devices)
    local_terms = lax.dot_general(
        queries, adapted_grad, (((0,), (0,)), ((), ())), preferred_element_type=jnp.float32
    )
    group_terms = lax.psum(local_terms.astype(jnp.bfloat16), "rep").astype(jnp.float32)
    summed = lax.psum_scatter(group_terms, "docs", scatter_dimension=0, tiled=True)
    adapter_grad = (summed * inverse_root).astype(jnp.bfloat16)
    return (losses, query_grads, adapter_grad)


def dot_nt(a, b):
    return lax.dot_general(a, b, (((1,), (1,)), ((), ())), preferred_element_type=jnp.float32)


def dot_tn(a, b):
    return lax.dot_general(a, b, (((0,), (0,)), ((), ())), preferred_element_type=jnp.float32)


def ring_group(position, groups):
    column = position // (groups // 2)
    along = position + column * (groups - 1 - 2 * position)
    return 2 * along + column


def gathered_kernel(
    groups, reps, fanout, per_owner, inverse_root,
    queries_ref, adapter_hbm, doc_hbm, routes_hbm, doc_rows_hbm, labels_hbm,
    loss_ref, query_grad_ref, adapter_grad_ref,
    adapter_ref, doc_ref, docs_all, unit_all, raw_all, meta_all, routes_all, radius_all,
    marks_all, score_ref, weight_ref, sums, label_sum, stats, stats_in,
    pair_out, pair_in, cross_out, cross_in, near_out, near_in, pull_ref,
    project_out, project_in, grad_cols, grad_home,
    terms_out, terms_in, final_cols,
    load_sem, ring_send, ring_recv, rep_send, rep_recv, pull_send, pull_recv,
    terms_send, terms_recv, final_send, final_recv,
):
    docs_at = lax.axis_index("docs")
    rep_at = lax.axis_index("rep")
    rows, width = queries_ref.shape
    doc_count = doc_ref.shape[0]
    half = doc_count // 2
    others = reps - 1
    candidates = fanout * per_owner
    score_scale = 2.0 / math.sqrt(width)
    pull_scale = LOSS_SCALE * score_scale
    block = width // reps
    all_rows = reps * rows

    loads = [
        pltpu.make_async_copy(source, landing, load_sem.at[at])
        for at, (source, landing) in enumerate(
            (
                (doc_hbm, doc_ref),
                (queries_ref, raw_all.at[rep_at]),
                (adapter_hbm, adapter_ref),
                (routes_hbm, routes_all.at[rep_at]),
                (doc_rows_hbm, meta_all.at[rep_at, pl.ds(0, candidates)]),
                (labels_hbm, meta_all.at[rep_at, pl.ds(candidates, candidates)]),
            )
        )
    ]
    for load in loads:
        load.start()

    def rep_peer(step):
        return lax.rem(rep_at + step, reps)

    pair = rep_at + 1 - 2 * lax.rem(rep_at, 2)
    cross = rep_peer(2)
    pair_cross = lax.rem(pair + 2, reps)

    along, column = docs_at // 2, docs_at % 2
    place = along + column * (groups - 1 - 2 * along)
    right = ring_group(lax.rem(place + 1, groups), groups)
    left = ring_group(lax.rem(place + groups - 1, groups), groups)

    barrier = pltpu.get_barrier_semaphore()
    for step in range(1, reps):
        pl.semaphore_signal(
            barrier, inc=1, device_id=(docs_at, rep_peer(step)), device_id_type=MESH
        )
    for step in range(1, groups):
        pl.semaphore_signal(
            barrier, inc=1, device_id=(lax.rem(docs_at + step, groups), rep_at), device_id_type=MESH
        )
    loads[0].wait()
    docs_all[0] = unit_rows(doc_ref[...])
    pl.semaphore_wait(barrier, others + groups - 1)

    def ring_copy(way, index):
        hop = index // 2
        if way == 0:
            part, source, landing, device = index % 2, hop, hop + 1, right
        else:
            part, source, landing, device = (
                1 - index % 2, (groups - hop) % groups, groups - hop - 1, left
            )
        return pltpu.make_async_remote_copy(
            src_ref=docs_all.at[source, pl.ds(part * half, half)],
            dst_ref=docs_all.at[landing, pl.ds(part * half, half)],
            send_sem=ring_send.at[way, index],
            recv_sem=ring_recv.at[way, index],
            device_id=(device, rep_at),
            device_id_type=MESH,
        )

    ring_steps = groups - 1
    for index in range(2):
        for way in range(2):
            ring_copy(way, index).start()

    def rep_copies(kind, source, landing):
        return [
            pltpu.make_async_remote_copy(
                src_ref=source(rep_peer(at + 1)),
                dst_ref=landing(at),
                send_sem=rep_send.at[kind, at],
                recv_sem=rep_recv.at[kind, at],
                device_id=(docs_at, rep_peer(at + 1)),
                device_id_type=MESH,
            )
            for at in range(others)
        ]

    def own_block(ref):
        return lambda at: ref.at[rep_at]

    for load in loads[3:]:
        load.wait()
    meta_copies = rep_copies(0, own_block(meta_all), own_block(meta_all)) + rep_copies(
        7, own_block(routes_all), own_block(routes_all)
    )
    for copy in meta_copies:
        copy.start()
    loads[1].wait()
    loads[2].wait()
    adapted = jnp.dot(raw_all[rep_at], adapter_ref[...], preferred_element_type=jnp.float32)
    radius = jnp.sqrt(jnp.mean(adapted * adapted, axis=-1, keepdims=True) + EPSILON)
    unit_all[rep_at] = (adapted / radius).astype(jnp.bfloat16)
    radius_all[rep_at] = jnp.broadcast_to(radius, (rows, 128))
    unit_copies = rep_copies(1, own_block(unit_all), own_block(unit_all))
    radius_copies = rep_copies(2, own_block(radius_all), own_block(radius_all))
    raw_copies = rep_copies(3, own_block(raw_all), own_block(raw_all))
    for copy in unit_copies + radius_copies + raw_copies:
        copy.start()
    stats[...] = jnp.zeros_like(stats)

    tile = 64
    tiles = doc_count // tile

    def label_mask(slot):
        owner = ring_group(lax.rem(place + groups - slot, groups), groups) * reps + rep_at

        def step(index, carry):
            at = index // tiles
            first = pl.multiple_of((index % tiles) * tile, tile)
            lanes = pl.ds(pl.multiple_of(at * rows, rows), rows)
            owners = routes_all[at]
            ids = jnp.full((per_owner, rows), -1, jnp.int32)
            marks = jnp.zeros((per_owner, rows), jnp.int32)
            for k in range(fanout):
                named = owners[k : k + 1, :] == owner
                ids = jnp.where(named, meta_all[at, k * per_owner : (k + 1) * per_owner, :], ids)
                low = candidates + k * per_owner
                marks = jnp.where(named, meta_all[at, low : low + per_owner, :] + 1, marks)
            marks = marks.astype(jnp.float32)
            here = lax.broadcasted_iota(jnp.int32, (tile, rows), 0) + first
            found = jnp.zeros((tile, rows), jnp.float32)
            for m in range(per_owner):
                found = jnp.where(here == ids[m : m + 1, :], marks[m : m + 1, :], found)
            marks_all[slot, pl.ds(first, tile), lanes] = found
            return carry

        lax.fori_loop(0, reps * tiles, step, 0)

    def score(slot):
        score_ref[...] = (
            dot_nt(docs_all[slot], unit_all[...].reshape(all_rows, width)) * score_scale
        )
        for at in range(reps):
            lanes = pl.ds(at * rows, rows)

            def step(index, totals):
                span = pl.ds(pl.multiple_of(index * tile, tile), tile)
                marks = marks_all[slot, span, lanes]
                scores = score_ref[span, lanes]
                held = marks > 0.5
                raised = jnp.where(held, jnp.exp(scores), 0.0)
                target = jnp.where(held, jnp.exp(marks - 1.0), 0.0) * label_sum[at, 0:1, :]
                weight_ref[0, span, lanes] = raised.astype(jnp.bfloat16)
                weight_ref[1, span, lanes] = (target * pull_scale).astype(jnp.bfloat16)
                return (
                    totals[0] + jnp.sum(raised, axis=0, keepdims=True),
                    totals[1] + jnp.sum(target * scores, axis=0, keepdims=True),
                )

            zero = jnp.zeros((1, rows), jnp.float32)
            norm, dotted = lax.fori_loop(0, tiles, step, (zero, zero))
            stats[at, 0:1, :] += norm
            stats[at, 1:2, :] += dotted

    def accumulate(slot, first):
        for kind in range(2):
            turned = weight_ref[kind].T
            for at in range(reps):
                term = jnp.dot(
                    turned,
                    docs_all[slot, :, at * block : (at + 1) * block],
                    preferred_element_type=jnp.float32,
                )
                if first:
                    sums[at, kind] = term
                else:
                    sums[at, kind] += term

    for index in range(ring_steps):
        for way in range(2):
            ring_copy(way, index).wait_recv()
            if index + 2 < ring_steps:
                ring_copy(way, index + 2).start()
        if index == 0:
            for copy in meta_copies:
                copy.wait_recv()
            for at in range(reps):
                raised_labels = jnp.exp(
                    meta_all[at, candidates : 2 * candidates, :].astype(jnp.float32)
                )
                label_sum[at, 0:1, :] = 1.0 / jnp.sum(raised_labels, axis=0, keepdims=True)
            for slot in range(4):
                label_mask(slot)
        elif index == 1:
            for slot in range(4, groups):
                label_mask(slot)
        elif index == 2:
            for copy in unit_copies:
                copy.wait_recv()
            for slot in (0, 1):
                score(slot)
                accumulate(slot, slot == 0)
        elif index == 3:
            score(groups - 1)
            accumulate(groups - 1, False)
        elif index % 2 == 0:
            for slot in (index // 2, groups - index // 2):
                score(slot)
                accumulate(slot, False)
    score(groups // 2)
    stat_copies = rep_copies(4, lambda at: stats, lambda at: stats_in.at[at])
    for copy in stat_copies:
        copy.start()
    accumulate(groups // 2, False)

    def pull_copy(at, source, landing, peer):
        return pltpu.make_async_remote_copy(
            src_ref=source,
            dst_ref=landing,
            send_sem=pull_send.at[at],
            recv_sem=pull_recv.at[at],
            device_id=(docs_at, peer),
            device_id_type=MESH,
        )

    pair_out[...] = sums[pair_cross].astype(jnp.bfloat16)
    pair_copy = pull_copy(0, pair_out, pair_in, pair)
    pair_copy.start()
    for copy in stat_copies:
        copy.wait_recv()
    shares = []
    for at in range(reps):
        total = stats[at]
        for origin in range(others):
            total = total + stats_in[origin, at]
        stats_in[0, at] = total
        shares.append((pull_scale / total).T[:, 0:1])
    own_stats = stats_in[0, rep_at]
    loss_ref[...] = jnp.log(own_stats[0:1, :]) - own_stats[1:2, :]
    pair_copy.wait_recv()
    cross_copies = []
    for at in range(reps):
        span = pl.ds(at * rows, rows)
        raised = sums[cross, 0, span, :] + pair_in[0, span, :].astype(jnp.float32)
        target = sums[cross, 1, span, :] + pair_in[1, span, :].astype(jnp.float32)
        cross_out[at] = (raised * shares[at] - target).astype(jnp.bfloat16)
        copy = pull_copy(2 + at, cross_out.at[at], cross_in.at[at], cross)
        copy.start()
        cross_copies.append(copy)
    for at in range(reps):
        span = pl.ds(at * rows, rows)
        near_out[at] = (sums[pair, 0, span, :] * shares[at] - sums[pair, 1, span, :]).astype(
            jnp.bfloat16
        )
    near_copy = pull_copy(1, near_out, near_in, pair)
    near_copy.start()
    for at in range(reps):
        span = pl.ds(at * rows, rows)
        pull_ref[at] = sums[rep_at, 0, span, :] * shares[at] - sums[rep_at, 1, span, :]
    near_copy.wait_recv()
    ones = jnp.ones((8, block), jnp.bfloat16)
    own_cols = pl.ds(pl.multiple_of(rep_at * block, block), block)
    for at in range(reps):
        held = pull_ref[at] + near_in[at].astype(jnp.float32)
        cross_copies[at].wait_recv()
        held = held + cross_in[at].astype(jnp.float32)
        pull_ref[at] = held
        unit = unit_all[at, :, own_cols].astype(jnp.float32)
        project_out[at] = dot_nt(ones, (unit * held).astype(jnp.bfloat16))
    project_copies = rep_copies(5, lambda at: project_out, lambda at: project_in.at[at])
    for copy in project_copies:
        copy.start()
    for copy in radius_copies + raw_copies + project_copies:
        copy.wait_recv()
    for at in range(reps):
        total = project_out[at]
        for origin in range(others):
            total = total + project_in[origin, at]
        projection = (total * (1.0 / width)).T[:, 0:1]
        unit = unit_all[at, :, own_cols].astype(jnp.float32)
        grad_cols[at] = ((pull_ref[at] - unit * projection) / radius_all[at, :, 0:1]).astype(
            jnp.bfloat16
        )
    grad_copies = rep_copies(6, lambda peer: grad_cols.at[peer], own_block(grad_home))
    for copy in grad_copies:
        copy.start()
    grad_home[rep_at] = grad_cols[rep_at]

    out_rows = width // groups
    parts = 2
    piece = block // parts
    group_terms = dot_tn(
        raw_all[...].reshape(all_rows, width), grad_cols[...].reshape(all_rows, block)
    ).astype(jnp.bfloat16).reshape(groups, out_rows, block)
    for part in range(parts):
        terms_out[part] = group_terms[:, :, part * piece : (part + 1) * piece]
    far_first = sorted(range(1, groups), key=lambda step: abs(step - groups // 2))
    term_copies = []
    for part in range(parts):
        for step in far_first:
            peer = lax.rem(docs_at + step, groups)
            copy = pltpu.make_async_remote_copy(
                src_ref=terms_out.at[part, peer],
                dst_ref=terms_in.at[part, step - 1],
                send_sem=terms_send.at[part, step - 1],
                recv_sem=terms_recv.at[part, step - 1],
                device_id=(peer, rep_at),
                device_id_type=MESH,
            )
            copy.start()
            term_copies.append(copy)
    for copy in grad_copies:
        copy.wait_recv()
    query_grad = dot_nt(grad_home[0], adapter_ref[:, 0:block])
    for at in range(1, reps):
        query_grad += dot_nt(grad_home[at], adapter_ref[:, at * block : (at + 1) * block])
    query_grad_ref[...] = query_grad.astype(jnp.bfloat16)
    final_copies = []
    for part in range(parts):
        summed = terms_out[part, docs_at].astype(jnp.float32)
        for at in range(groups - 1):
            term_copies[part * (groups - 1) + at].wait_recv()
        for at in range(groups - 1):
            summed = summed + terms_in[part, at].astype(jnp.float32)
        final_cols[part, rep_at] = (summed * inverse_root).astype(jnp.bfloat16)
        for at in range(others):
            copy = pltpu.make_async_remote_copy(
                src_ref=final_cols.at[part, rep_at],
                dst_ref=final_cols.at[part, rep_at],
                send_sem=final_send.at[part, at],
                recv_sem=final_recv.at[part, at],
                device_id=(docs_at, rep_peer(at + 1)),
                device_id_type=MESH,
            )
            copy.start()
            final_copies.append(copy)
    for part in range(parts):
        for at in range(others):
            final_copies[part * others + at].wait_recv()
        for at in range(reps):
            low = at * block + part * piece
            adapter_grad_ref[:, low : low + piece] = final_cols[part, at]

    for index in range(ring_steps):
        for way in range(2):
            ring_copy(way, index).wait_send()
    for copy in (
        meta_copies + unit_copies + radius_copies + raw_copies + stat_copies
        + [pair_copy, near_copy] + cross_copies + project_copies + grad_copies
        + term_copies + final_copies
    ):
        copy.wait_send()


def gathered_on_device(queries, adapter, doc_table, routes, doc_rows, labels):
    groups = lax.axis_size("docs")
    reps = lax.axis_size("rep")
    rows, width = queries.shape
    fanout = routes.shape[1]
    per_owner = doc_rows.shape[2]
    doc_count = doc_table.shape[0]
    candidates = fanout * per_owner
    block = width // reps
    out_rows = width // groups
    others = reps - 1
    all_rows = reps * rows
    bf16, f32 = jnp.bfloat16, jnp.float32
    vmem = pltpu.VMEM
    dma = pltpu.SemaphoreType.DMA
    losses, query_grads, adapter_grad = pl.pallas_call(
        functools.partial(
            gathered_kernel, groups, reps, fanout, per_owner,
            1.0 / math.sqrt(rows * groups * reps),
        ),
        out_shape=(
            jax.ShapeDtypeStruct((1, rows), f32),
            jax.ShapeDtypeStruct((rows, width), bf16),
            jax.ShapeDtypeStruct((out_rows, width), bf16),
        ),
        in_specs=[pl.BlockSpec(memory_space=pl.ANY)] * 6,
        out_specs=[pl.BlockSpec(memory_space=vmem)] * 3,
        scratch_shapes=[
            vmem((width, width), bf16),
            vmem((doc_count, width), bf16),
            vmem((groups, doc_count, width), bf16),
            vmem((reps, rows, width), bf16),
            vmem((reps, rows, width), bf16),
            vmem((reps, 2 * candidates, rows), jnp.int32),
            vmem((reps, fanout, rows), jnp.int32),
            vmem((reps, rows, 128), f32),
            vmem((groups, doc_count, all_rows), f32),
            vmem((doc_count, all_rows), f32),
            vmem((2, doc_count, all_rows), bf16),
            vmem((reps, 2, all_rows, block), f32),
            vmem((reps, 8, rows), f32),
            vmem((reps, 8, rows), f32),
            vmem((others, reps, 8, rows), f32),
            vmem((2, all_rows, block), bf16),
            vmem((2, all_rows, block), bf16),
            vmem((reps, rows, block), bf16),
            vmem((reps, rows, block), bf16),
            vmem((reps, rows, block), bf16),
            vmem((reps, rows, block), bf16),
            vmem((reps, rows, block), f32),
            vmem((reps, 8, rows), f32),
            vmem((others, reps, 8, rows), f32),
            vmem((reps, rows, block), bf16),
            vmem((reps, rows, block), bf16),
            vmem((2, groups, out_rows, block // 2), bf16),
            vmem((2, groups - 1, out_rows, block // 2), bf16),
            vmem((2, reps, out_rows, block // 2), bf16),
            dma((6,)),
            dma((2, groups - 1)),
            dma((2, groups - 1)),
            dma((8, others)),
            dma((8, others)),
            dma((2 + reps,)),
            dma((2 + reps,)),
            dma((2, groups - 1)),
            dma((2, groups - 1)),
            dma((2, others)),
            dma((2, others)),
        ],
        compiler_params=pltpu.CompilerParams(
            collective_id=0, has_side_effects=True, vmem_limit_bytes=56 * 1024 * 1024
        ),
    )(
        queries, adapter, doc_table, routes.T,
        doc_rows.reshape(rows, candidates).T, labels.reshape(rows, candidates).T,
    )
    return (losses.reshape(rows), query_grads, adapter_grad)


def on_device(queries, adapter, doc_table, routes, doc_rows, labels):
    gathered_bytes = lax.axis_size("docs") * doc_table.size * doc_table.dtype.itemsize
    if gathered_bytes <= GATHER_LIMIT and lax.axis_size("rep") == 4:
        return gathered_on_device(queries, adapter, doc_table, routes, doc_rows, labels)
    return routed_on_device(queries, adapter, doc_table, routes, doc_rows, labels)


def solution(mesh):
    placed = (
        P(("docs", "rep"), None),
        P(),
        P(("docs", "rep"), None),
        P(("docs", "rep"), None),
        P(("docs", "rep"), None, None),
        P(("docs", "rep"), None, None),
    )
    return jax.shard_map(
        on_device,
        mesh=mesh,
        in_specs=placed,
        out_specs=(P(("docs", "rep")), P(("docs", "rep"), None), P("docs", None)),
        check_vma=False,
    )
```

```python
import functools
import math

import jax
import jax.numpy as jnp
from jax import lax
from jax.experimental import pallas as pl
from jax.experimental.pallas import tpu as pltpu
from jax.sharding import PartitionSpec as P

EPSILON = 1e-06
LOSS_SCALE = 128.0
MESH = pl.DeviceIdType.MESH
GATHER_LIMIT = 8 * 1024 * 1024


def unit_rows(rows):
    widened = rows.astype(jnp.float32)
    return (
        widened / jnp.sqrt(jnp.mean(widened * widened, axis=-1, keepdims=True) + EPSILON)
    ).astype(jnp.bfloat16)


def routed_on_device(queries, adapter, doc_table, routes, doc_rows, labels):
    doc_groups = lax.axis_size("docs")
    rep_groups = lax.axis_size("rep")
    devices = doc_groups * rep_groups
    query_rows, feature_width = queries.shape
    fanout = routes.shape[1]
    per_owner = doc_rows.shape[2]
    doc_count = doc_table.shape[0]
    capacity = max(2, 2 * query_rows * fanout // devices)
    slots_all = devices * capacity
    score_scale = 2.0 / math.sqrt(feature_width)
    adapted = jnp.dot(queries, adapter, preferred_element_type=jnp.float32)
    radius = jnp.sqrt(jnp.mean(adapted * adapted, axis=-1, keepdims=True) + EPSILON)
    unit_exact = adapted / radius
    unit_query = unit_exact.astype(jnp.bfloat16)
    owner_hits = (routes[:, :, None] == jnp.arange(devices, dtype=jnp.int32)[None, None, :]).astype(
        jnp.int32
    )
    per_query = jnp.sum(owner_hits, axis=1)
    row_index = jnp.arange(query_rows, dtype=jnp.int32)
    lower_table = (row_index[:, None] > row_index[None, :]).astype(jnp.float32)
    earlier = jnp.dot(
        lower_table, per_query.astype(jnp.float32), precision=lax.Precision.HIGHEST
    ).astype(jnp.int32)
    slot_index = jnp.sum(earlier[:, None, :] * owner_hits, axis=-1)
    placed = routes * capacity + slot_index
    target_slot = placed.reshape(-1)
    repeated = jnp.broadcast_to(
        unit_query[:, None, :], (query_rows, fanout, feature_width)
    ).reshape(-1, feature_width)
    outgoing = jnp.zeros((slots_all, feature_width), jnp.bfloat16).at[target_slot].set(repeated)
    outgoing_ids = (
        jnp.zeros((slots_all, per_owner), jnp.int32)
        .at[target_slot]
        .set(doc_rows.reshape(-1, per_owner))
    )
    outgoing = outgoing.reshape(doc_groups, rep_groups, capacity, feature_width)
    outgoing_ids = outgoing_ids.reshape(doc_groups, rep_groups, capacity, per_owner)
    arrived, arrived_ids = (
        lax.all_to_all(
            lax.all_to_all(outgoing, "docs", split_axis=0, concat_axis=0, tiled=True),
            "rep",
            split_axis=1,
            concat_axis=1,
            tiled=True,
        ),
        lax.all_to_all(
            lax.all_to_all(outgoing_ids, "docs", split_axis=0, concat_axis=0, tiled=True),
            "rep",
            split_axis=1,
            concat_axis=1,
            tiled=True,
        ),
    )
    arrived = arrived.reshape(slots_all, feature_width)
    arrived_ids = arrived_ids.reshape(slots_all, per_owner)
    doc_unit = unit_rows(doc_table)
    block_scores = lax.dot_general(
        arrived, doc_unit, (((1,), (1,)), ((), ())), preferred_element_type=jnp.float32
    )
    scores_out = jnp.take_along_axis(block_scores, arrived_ids, axis=1) * score_scale
    returned = lax.all_to_all(
        lax.all_to_all(
            scores_out.reshape(doc_groups, rep_groups, capacity, per_owner).astype(jnp.bfloat16),
            "docs",
            split_axis=0,
            concat_axis=0,
            tiled=True,
        ),
        "rep",
        split_axis=1,
        concat_axis=1,
        tiled=True,
    ).astype(jnp.float32)
    scores = returned.reshape(slots_all, per_owner)[placed]
    raised = jnp.exp(scores)
    norm_total = jnp.sum(raised, axis=(1, 2))
    label_weight = jnp.exp(labels.astype(jnp.float32))
    target = label_weight / jnp.sum(label_weight, axis=(1, 2), keepdims=True)
    losses = jnp.log(norm_total) - jnp.sum(target * scores, axis=(1, 2))
    weights = (LOSS_SCALE * (raised / norm_total[:, None, None] - target)).astype(jnp.bfloat16)
    weight_slots = (
        jnp.zeros((slots_all, per_owner), jnp.bfloat16)
        .at[target_slot]
        .set(weights.reshape(-1, per_owner))
    )
    weights_in = lax.all_to_all(
        lax.all_to_all(
            weight_slots.reshape(doc_groups, rep_groups, capacity, per_owner),
            "docs",
            split_axis=0,
            concat_axis=0,
            tiled=True,
        ),
        "rep",
        split_axis=1,
        concat_axis=1,
        tiled=True,
    )
    weights_in = weights_in.reshape(slots_all, per_owner)
    spread = (
        jnp.zeros((slots_all, doc_count), jnp.bfloat16)
        .at[jnp.arange(slots_all)[:, None], arrived_ids]
        .set(weights_in)
    )
    pull_out = (jnp.dot(spread, doc_unit, preferred_element_type=jnp.float32) * score_scale).astype(
        jnp.bfloat16
    )
    pull_out = pull_out.reshape(doc_groups, rep_groups, capacity, feature_width)
    pull_back = lax.all_to_all(
        lax.all_to_all(pull_out, "docs", split_axis=0, concat_axis=0, tiled=True),
        "rep",
        split_axis=1,
        concat_axis=1,
        tiled=True,
    )
    pull_rows = pull_back.reshape(slots_all, feature_width)[placed]
    pull_total = jnp.sum(pull_rows.astype(jnp.float32), axis=1)
    projection = jnp.mean(unit_exact * pull_total, axis=-1, keepdims=True)
    adapted_grad = ((pull_total - unit_exact * projection) / radius).astype(jnp.bfloat16)
    query_grads = lax.dot_general(
        adapted_grad, adapter, (((1,), (1,)), ((), ())), preferred_element_type=jnp.float32
    ).astype(jnp.bfloat16)
    inverse_root = 1.0 / math.sqrt(query_rows * devices)
    local_terms = lax.dot_general(
        queries, adapted_grad, (((0,), (0,)), ((), ())), preferred_element_type=jnp.float32
    )
    group_terms = lax.psum(local_terms.astype(jnp.bfloat16), "rep").astype(jnp.float32)
    summed = lax.psum_scatter(group_terms, "docs", scatter_dimension=0, tiled=True)
    adapter_grad = (summed * inverse_root).astype(jnp.bfloat16)
    return (losses, query_grads, adapter_grad)


def dot_nt(a, b):
    return lax.dot_general(a, b, (((1,), (1,)), ((), ())), preferred_element_type=jnp.float32)


def ring_group(position, groups):
    column = position // (groups // 2)
    along = position + column * (groups - 1 - 2 * position)
    return 2 * along + column


def gathered_kernel(
    groups, reps, fanout, per_owner, inverse_root,
    queries_ref, adapter_hbm, doc_hbm, meta_hbm,
    loss_ref, query_grad_ref, adapter_grad_ref,
    adapter_ref, doc_ref, docs_all, unit_all, raw_all, meta_all, radius_all,
    marks_all, here_ref, raw_turned, score_ref, weight_ref, sums, label_sum, stats, stats_in,
    pair_out, pair_in, cross_out, cross_in, near_out, near_in, pull_ref,
    project_out, project_in, grad_cols, grad_home,
    terms_out, terms_in, final_cols,
    load_sem, ring_send, ring_recv, rep_send, rep_recv, pull_send, pull_recv,
    terms_send, terms_recv, final_send, final_recv,
):
    docs_at = lax.axis_index("docs")
    rep_at = lax.axis_index("rep")
    rows, width = queries_ref.shape
    doc_count = doc_ref.shape[0]
    half = doc_count // 2
    others = reps - 1
    candidates = fanout * per_owner
    score_scale = 2.0 / math.sqrt(width)
    pull_scale = LOSS_SCALE * score_scale
    block = width // reps
    all_rows = reps * rows

    loads = [
        pltpu.make_async_copy(source, landing, load_sem.at[at])
        for at, (source, landing) in enumerate(
            (
                (doc_hbm, doc_ref),
                (queries_ref, raw_all.at[rep_at]),
                (adapter_hbm, adapter_ref),
                (meta_hbm, meta_all.at[rep_at]),
            )
        )
    ]
    for load in loads:
        load.start()

    def rep_peer(step):
        return lax.rem(rep_at + step, reps)

    pair = rep_at + 1 - 2 * lax.rem(rep_at, 2)
    cross = rep_peer(2)
    pair_cross = lax.rem(pair + 2, reps)

    along, column = docs_at // 2, docs_at % 2
    place = along + column * (groups - 1 - 2 * along)
    right = ring_group(lax.rem(place + 1, groups), groups)
    left = ring_group(lax.rem(place + groups - 1, groups), groups)

    barrier = pltpu.get_barrier_semaphore()
    for step in range(1, reps):
        pl.semaphore_signal(
            barrier, inc=1, device_id=(docs_at, rep_peer(step)), device_id_type=MESH
        )
    for step in range(1, groups):
        pl.semaphore_signal(
            barrier, inc=1, device_id=(lax.rem(docs_at + step, groups), rep_at), device_id_type=MESH
        )
    loads[0].wait()
    docs_all[0] = unit_rows(doc_ref[...])
    pl.semaphore_wait(barrier, others + groups - 1)

    def ring_copy(way, index):
        hop = index // 2
        if way == 0:
            part, source, landing, device = index % 2, hop, hop + 1, right
        else:
            part, source, landing, device = (
                1 - index % 2, (groups - hop) % groups, groups - hop - 1, left
            )
        return pltpu.make_async_remote_copy(
            src_ref=docs_all.at[source, pl.ds(part * half, half)],
            dst_ref=docs_all.at[landing, pl.ds(part * half, half)],
            send_sem=ring_send.at[way, index],
            recv_sem=ring_recv.at[way, index],
            device_id=(device, rep_at),
            device_id_type=MESH,
        )

    ring_steps = groups - 1
    for index in range(2):
        for way in range(2):
            ring_copy(way, index).start()

    def rep_copies(kind, source, landing):
        return [
            pltpu.make_async_remote_copy(
                src_ref=source(rep_peer(at + 1)),
                dst_ref=landing(at),
                send_sem=rep_send.at[kind, at],
                recv_sem=rep_recv.at[kind, at],
                device_id=(docs_at, rep_peer(at + 1)),
                device_id_type=MESH,
            )
            for at in range(others)
        ]

    def own_block(ref):
        return lambda at: ref.at[rep_at]

    loads[3].wait()
    meta_copies = rep_copies(0, own_block(meta_all), own_block(meta_all))
    for copy in meta_copies:
        copy.start()
    loads[1].wait()
    loads[2].wait()
    adapted = jnp.dot(raw_all[rep_at], adapter_ref[...], preferred_element_type=jnp.float32)
    radius = jnp.sqrt(jnp.mean(adapted * adapted, axis=-1, keepdims=True) + EPSILON)
    unit_all[rep_at] = (adapted / radius).astype(jnp.bfloat16)
    radius_all[rep_at] = jnp.broadcast_to(radius, (rows, 128))
    unit_copies = rep_copies(1, own_block(unit_all), own_block(unit_all))
    radius_copies = rep_copies(2, own_block(radius_all), own_block(radius_all))
    raw_copies = rep_copies(3, own_block(raw_all), own_block(raw_all))
    for copy in unit_copies + radius_copies:
        copy.start()
    stats[...] = jnp.zeros_like(stats)
    here_ref[...] = (
        lax.broadcasted_iota(jnp.int32, (doc_count, rows), 0).astype(jnp.float32).astype(jnp.bfloat16)
    )

    tile = 64
    tiles = doc_count // tile

    def label_mask(slot):
        owner = ring_group(lax.rem(place + groups - slot, groups), groups) * reps + rep_at

        def step(index, carry):
            at = index // tiles
            first = pl.multiple_of((index % tiles) * tile, tile)
            lanes = pl.ds(pl.multiple_of(at * rows, rows), rows)
            owners = meta_all[at, 2 * candidates : 2 * candidates + 8, :]
            ids = jnp.full((per_owner, rows), -1, jnp.int32)
            marks = jnp.zeros((per_owner, rows), jnp.int32)
            for k in range(fanout):
                named = owners[k : k + 1, :] == owner
                ids = jnp.where(named, meta_all[at, k * per_owner : (k + 1) * per_owner, :], ids)
                low = candidates + k * per_owner
                marks = jnp.where(named, meta_all[at, low : low + per_owner, :] + 1, marks)
            ids = ids.astype(jnp.float32).astype(jnp.bfloat16)
            marks = marks.astype(jnp.float32).astype(jnp.bfloat16)
            here = here_ref[pl.ds(first, tile), :]
            found = jnp.zeros((tile, rows), jnp.bfloat16)
            for m in range(per_owner):
                found = jnp.where(here == ids[m : m + 1, :], marks[m : m + 1, :], found)
            marks_all[slot, pl.ds(first, tile), lanes] = found
            return carry

        lax.fori_loop(0, reps * tiles, step, 0)

    def score(slot, buffer):
        score_ref[...] = (
            dot_nt(docs_all[slot], unit_all[...].reshape(all_rows, width)) * score_scale
        )
        for at in range(reps):
            lanes = pl.ds(at * rows, rows)

            def step(index, totals):
                span = pl.ds(pl.multiple_of(index * tile, tile), tile)
                marks = marks_all[slot, span, lanes].astype(jnp.float32)
                scores = score_ref[span, lanes]
                held = marks > 0.5
                raised = jnp.where(held, jnp.exp(scores), 0.0)
                target = jnp.where(held, jnp.exp(marks - 1.0), 0.0) * label_sum[at, 0:1, :]
                weight_ref[buffer, 0, span, lanes] = raised.astype(jnp.bfloat16)
                weight_ref[buffer, 1, span, lanes] = (target * pull_scale).astype(jnp.bfloat16)
                return (
                    totals[0] + jnp.sum(raised, axis=0, keepdims=True),
                    totals[1] + jnp.sum(target * scores, axis=0, keepdims=True),
                )

            zero = jnp.zeros((1, rows), jnp.float32)
            norm, dotted = lax.fori_loop(0, tiles, step, (zero, zero))
            stats[at, 0:1, :] += norm
            stats[at, 1:2, :] += dotted

    def accumulate(slots, first):
        for kind in range(2):
            turned = [weight_ref[buffer, kind].T for buffer in range(len(slots))]
            for at in range(reps):
                terms = [
                    jnp.dot(
                        part,
                        docs_all[slot, :, at * block : (at + 1) * block],
                        preferred_element_type=jnp.float32,
                    )
                    for part, slot in zip(turned, slots)
                ]
                if first:
                    sums[at, kind] = sum(terms)
                else:
                    sums[at, kind] += sum(terms)

    def between(index, way):
        if index == 0 and way == 0:
            for copy in meta_copies:
                copy.wait_recv()
            for at in range(reps):
                raised_labels = jnp.exp(
                    meta_all[at, candidates : 2 * candidates, :].astype(jnp.float32)
                )
                label_sum[at, 0:1, :] = 1.0 / jnp.sum(raised_labels, axis=0, keepdims=True)
        if index < 2:
            share = groups // 4
            first = (2 * index + way) * share
            for slot in range(first, first + share):
                label_mask(slot)
        elif index == 2 and way == 0:
            for copy in unit_copies:
                copy.wait_recv()
            for copy in raw_copies:
                copy.start()
            score(0, 0)
            accumulate((0,), True)
        elif index == 2:
            score(1, 0)
        elif index == 3 and way == 0:
            score(groups - 1, 1)
            accumulate((1, groups - 1), False)
        elif index % 2 == 0 and way == 0 and index < ring_steps - 1:
            score(index // 2, 0)
        elif index % 2 == 0 and index < ring_steps - 1:
            score(groups - index // 2, 1)
            accumulate((index // 2, groups - index // 2), False)
        elif index == ring_steps - 2 and way == 0:
            score(groups // 2 - 1, 0)
        elif index == ring_steps - 2:
            score(groups // 2 + 1, 1)
            accumulate((groups // 2 - 1, groups // 2 + 1), False)
            for copy in raw_copies:
                copy.wait_recv()
            for at in range(reps):
                raw_turned[:, at * rows : (at + 1) * rows] = raw_all[at].T

    for index in range(ring_steps):
        for way in range(2):
            ring_copy(way, index).wait_recv()
            if index + 2 < ring_steps:
                ring_copy(way, index + 2).start()
            between(index, way)
    score(groups // 2, 0)
    stat_copies = rep_copies(4, lambda at: stats, lambda at: stats_in.at[at])
    for copy in stat_copies:
        copy.start()
    accumulate((groups // 2,), False)

    def pull_copy(at, source, landing, peer):
        return pltpu.make_async_remote_copy(
            src_ref=source,
            dst_ref=landing,
            send_sem=pull_send.at[at],
            recv_sem=pull_recv.at[at],
            device_id=(docs_at, peer),
            device_id_type=MESH,
        )

    pair_out[...] = sums[pair_cross].astype(jnp.bfloat16)
    pair_copy = pull_copy(0, pair_out, pair_in, pair)
    pair_copy.start()
    for copy in stat_copies:
        copy.wait_recv()
    shares = []
    for at in range(reps):
        total = stats[at]
        for origin in range(others):
            total = total + stats_in[origin, at]
        stats_in[0, at] = total
        shares.append((pull_scale / total).T[:, 0:1])
    own_stats = stats_in[0, rep_at]
    loss_ref[...] = jnp.log(own_stats[0:1, :]) - own_stats[1:2, :]
    pair_copy.wait_recv()
    cross_copies = []
    for at in range(reps):
        span = pl.ds(at * rows, rows)
        raised = sums[cross, 0, span, :] + pair_in[0, span, :].astype(jnp.float32)
        target = sums[cross, 1, span, :] + pair_in[1, span, :].astype(jnp.float32)
        cross_out[at] = (raised * shares[at] - target).astype(jnp.bfloat16)
        copy = pull_copy(2 + at, cross_out.at[at], cross_in.at[at], cross)
        copy.start()
        cross_copies.append(copy)
    for at in range(reps):
        span = pl.ds(at * rows, rows)
        near_out[at] = (sums[pair, 0, span, :] * shares[at] - sums[pair, 1, span, :]).astype(
            jnp.bfloat16
        )
    near_copy = pull_copy(1, near_out, near_in, pair)
    near_copy.start()
    for at in range(reps):
        span = pl.ds(at * rows, rows)
        pull_ref[at] = sums[rep_at, 0, span, :] * shares[at] - sums[rep_at, 1, span, :]
    near_copy.wait_recv()
    ones = jnp.ones((8, block), jnp.bfloat16)
    own_cols = pl.ds(pl.multiple_of(rep_at * block, block), block)
    for at in range(reps):
        held = pull_ref[at] + near_in[at].astype(jnp.float32)
        cross_copies[at].wait_recv()
        held = held + cross_in[at].astype(jnp.float32)
        pull_ref[at] = held
        unit = unit_all[at, :, own_cols].astype(jnp.float32)
        project_out[at] = dot_nt(ones, (unit * held).astype(jnp.bfloat16))
    project_copies = rep_copies(5, lambda at: project_out, lambda at: project_in.at[at])
    for copy in project_copies:
        copy.start()
    for copy in radius_copies + project_copies:
        copy.wait_recv()
    for at in range(reps):
        total = project_out[at]
        for origin in range(others):
            total = total + project_in[origin, at]
        projection = (total * (1.0 / width)).T[:, 0:1]
        unit = unit_all[at, :, own_cols].astype(jnp.float32)
        grad_cols[at] = ((pull_ref[at] - unit * projection) / radius_all[at, :, 0:1]).astype(
            jnp.bfloat16
        )
    grad_copies = rep_copies(6, lambda peer: grad_cols.at[peer], own_block(grad_home))
    for copy in grad_copies:
        copy.start()
    grad_home[rep_at] = grad_cols[rep_at]

    out_rows = width // groups
    parts = 2
    piece = block // parts
    group_terms = jnp.dot(
        raw_turned[...], grad_cols[...].reshape(all_rows, block), preferred_element_type=jnp.float32
    ).astype(jnp.bfloat16).reshape(groups, out_rows, block)
    for part in range(parts):
        terms_out[part] = group_terms[:, :, part * piece : (part + 1) * piece]
    far_first = sorted(range(1, groups), key=lambda step: abs(step - groups // 2))
    term_copies = []
    for part in range(parts):
        for step in far_first:
            peer = lax.rem(docs_at + step, groups)
            copy = pltpu.make_async_remote_copy(
                src_ref=terms_out.at[part, peer],
                dst_ref=terms_in.at[part, step - 1],
                send_sem=terms_send.at[part, step - 1],
                recv_sem=terms_recv.at[part, step - 1],
                device_id=(peer, rep_at),
                device_id_type=MESH,
            )
            copy.start()
            term_copies.append(copy)
    for copy in grad_copies:
        copy.wait_recv()
    query_grad = dot_nt(grad_home[0], adapter_ref[:, 0:block])
    for at in range(1, reps):
        query_grad += dot_nt(grad_home[at], adapter_ref[:, at * block : (at + 1) * block])
    query_grad_ref[...] = query_grad.astype(jnp.bfloat16)
    final_copies = []
    for part in range(parts):
        summed = terms_out[part, docs_at].astype(jnp.float32)
        for at in range(groups - 1):
            term_copies[part * (groups - 1) + at].wait_recv()
        for at in range(groups - 1):
            summed = summed + terms_in[part, at].astype(jnp.float32)
        final_cols[part, rep_at] = (summed * inverse_root).astype(jnp.bfloat16)
        for at in range(others):
            copy = pltpu.make_async_remote_copy(
                src_ref=final_cols.at[part, rep_at],
                dst_ref=final_cols.at[part, rep_at],
                send_sem=final_send.at[part, at],
                recv_sem=final_recv.at[part, at],
                device_id=(docs_at, rep_peer(at + 1)),
                device_id_type=MESH,
            )
            copy.start()
            final_copies.append(copy)
    for part in range(parts):
        for at in range(others):
            final_copies[part * others + at].wait_recv()
        for at in range(reps):
            low = at * block + part * piece
            adapter_grad_ref[:, low : low + piece] = final_cols[part, at]

    for index in range(ring_steps):
        for way in range(2):
            ring_copy(way, index).wait_send()
    for copy in (
        meta_copies + unit_copies + radius_copies + raw_copies + stat_copies
        + [pair_copy, near_copy] + cross_copies + project_copies + grad_copies
        + term_copies + final_copies
    ):
        copy.wait_send()


def gathered_on_device(queries, adapter, doc_table, routes, doc_rows, labels):
    groups = lax.axis_size("docs")
    reps = lax.axis_size("rep")
    rows, width = queries.shape
    fanout = routes.shape[1]
    per_owner = doc_rows.shape[2]
    doc_count = doc_table.shape[0]
    candidates = fanout * per_owner
    block = width // reps
    out_rows = width // groups
    others = reps - 1
    all_rows = reps * rows
    meta = jnp.concatenate(
        [
            doc_rows.reshape(rows, candidates),
            labels.reshape(rows, candidates),
            routes,
            jnp.zeros((rows, 8 - fanout), jnp.int32),
        ],
        axis=1,
    ).T
    bf16, f32 = jnp.bfloat16, jnp.float32
    vmem = pltpu.VMEM
    dma = pltpu.SemaphoreType.DMA
    losses, query_grads, adapter_grad = pl.pallas_call(
        functools.partial(
            gathered_kernel, groups, reps, fanout, per_owner,
            1.0 / math.sqrt(rows * groups * reps),
        ),
        out_shape=(
            jax.ShapeDtypeStruct((1, rows), f32),
            jax.ShapeDtypeStruct((rows, width), bf16),
            jax.ShapeDtypeStruct((out_rows, width), bf16),
        ),
        in_specs=[pl.BlockSpec(memory_space=pl.ANY)] * 4,
        out_specs=[pl.BlockSpec(memory_space=vmem)] * 3,
        scratch_shapes=[
            vmem((width, width), bf16),
            vmem((doc_count, width), bf16),
            vmem((groups, doc_count, width), bf16),
            vmem((reps, rows, width), bf16),
            vmem((reps, rows, width), bf16),
            vmem((reps, 2 * candidates + 8, rows), jnp.int32),
            vmem((reps, rows, 128), f32),
            vmem((groups, doc_count, all_rows), bf16),
            vmem((doc_count, rows), bf16),
            vmem((width, all_rows), bf16),
            vmem((doc_count, all_rows), f32),
            vmem((2, 2, doc_count, all_rows), bf16),
            vmem((reps, 2, all_rows, block), f32),
            vmem((reps, 8, rows), f32),
            vmem((reps, 8, rows), f32),
            vmem((others, reps, 8, rows), f32),
            vmem((2, all_rows, block), bf16),
            vmem((2, all_rows, block), bf16),
            vmem((reps, rows, block), bf16),
            vmem((reps, rows, block), bf16),
            vmem((reps, rows, block), bf16),
            vmem((reps, rows, block), bf16),
            vmem((reps, rows, block), f32),
            vmem((reps, 8, rows), f32),
            vmem((others, reps, 8, rows), f32),
            vmem((reps, rows, block), bf16),
            vmem((reps, rows, block), bf16),
            vmem((2, groups, out_rows, block // 2), bf16),
            vmem((2, groups - 1, out_rows, block // 2), bf16),
            vmem((2, reps, out_rows, block // 2), bf16),
            dma((4,)),
            dma((2, groups - 1)),
            dma((2, groups - 1)),
            dma((7, others)),
            dma((7, others)),
            dma((2 + reps,)),
            dma((2 + reps,)),
            dma((2, groups - 1)),
            dma((2, groups - 1)),
            dma((2, others)),
            dma((2, others)),
        ],
        compiler_params=pltpu.CompilerParams(
            collective_id=0, has_side_effects=True, vmem_limit_bytes=213 * 256 * 1024
        ),
    )(
        queries, adapter, doc_table, meta,
    )
    return (losses.reshape(rows), query_grads, adapter_grad)


def on_device(queries, adapter, doc_table, routes, doc_rows, labels):
    gathered_bytes = lax.axis_size("docs") * doc_table.size * doc_table.dtype.itemsize
    if gathered_bytes <= GATHER_LIMIT and lax.axis_size("rep") == 4:
        return gathered_on_device(queries, adapter, doc_table, routes, doc_rows, labels)
    return routed_on_device(queries, adapter, doc_table, routes, doc_rows, labels)


def solution(mesh):
    placed = (
        P(("docs", "rep"), None),
        P(),
        P(("docs", "rep"), None),
        P(("docs", "rep"), None),
        P(("docs", "rep"), None, None),
        P(("docs", "rep"), None, None),
    )
    return jax.shard_map(
        on_device,
        mesh=mesh,
        in_specs=placed,
        out_specs=(P(("docs", "rep")), P(("docs", "rep"), None), P("docs", None)),
        check_vma=False,
    )
```

```python
import functools
import math

import jax
import jax.numpy as jnp
from jax import lax
from jax.experimental import pallas as pl
from jax.experimental.pallas import tpu as pltpu
from jax.sharding import PartitionSpec as P

EPSILON = 1e-06
LOSS_SCALE = 128.0
MESH = pl.DeviceIdType.MESH
GATHER_LIMIT = 8 * 1024 * 1024


def unit_rows(rows):
    widened = rows.astype(jnp.float32)
    return (
        widened / jnp.sqrt(jnp.mean(widened * widened, axis=-1, keepdims=True) + EPSILON)
    ).astype(jnp.bfloat16)


def routed_on_device(queries, adapter, doc_table, routes, doc_rows, labels):
    doc_groups = lax.axis_size("docs")
    rep_groups = lax.axis_size("rep")
    devices = doc_groups * rep_groups
    query_rows, feature_width = queries.shape
    fanout = routes.shape[1]
    per_owner = doc_rows.shape[2]
    doc_count = doc_table.shape[0]
    capacity = max(2, 2 * query_rows * fanout // devices)
    slots_all = devices * capacity
    score_scale = 2.0 / math.sqrt(feature_width)
    adapted = jnp.dot(queries, adapter, preferred_element_type=jnp.float32)
    radius = jnp.sqrt(jnp.mean(adapted * adapted, axis=-1, keepdims=True) + EPSILON)
    unit_exact = adapted / radius
    unit_query = unit_exact.astype(jnp.bfloat16)
    owner_hits = (routes[:, :, None] == jnp.arange(devices, dtype=jnp.int32)[None, None, :]).astype(
        jnp.int32
    )
    per_query = jnp.sum(owner_hits, axis=1)
    row_index = jnp.arange(query_rows, dtype=jnp.int32)
    lower_table = (row_index[:, None] > row_index[None, :]).astype(jnp.float32)
    earlier = jnp.dot(
        lower_table, per_query.astype(jnp.float32), precision=lax.Precision.HIGHEST
    ).astype(jnp.int32)
    slot_index = jnp.sum(earlier[:, None, :] * owner_hits, axis=-1)
    placed = routes * capacity + slot_index
    target_slot = placed.reshape(-1)
    repeated = jnp.broadcast_to(
        unit_query[:, None, :], (query_rows, fanout, feature_width)
    ).reshape(-1, feature_width)
    outgoing = jnp.zeros((slots_all, feature_width), jnp.bfloat16).at[target_slot].set(repeated)
    outgoing_ids = (
        jnp.zeros((slots_all, per_owner), jnp.int32)
        .at[target_slot]
        .set(doc_rows.reshape(-1, per_owner))
    )
    outgoing = outgoing.reshape(doc_groups, rep_groups, capacity, feature_width)
    outgoing_ids = outgoing_ids.reshape(doc_groups, rep_groups, capacity, per_owner)
    arrived, arrived_ids = (
        lax.all_to_all(
            lax.all_to_all(outgoing, "docs", split_axis=0, concat_axis=0, tiled=True),
            "rep",
            split_axis=1,
            concat_axis=1,
            tiled=True,
        ),
        lax.all_to_all(
            lax.all_to_all(outgoing_ids, "docs", split_axis=0, concat_axis=0, tiled=True),
            "rep",
            split_axis=1,
            concat_axis=1,
            tiled=True,
        ),
    )
    arrived = arrived.reshape(slots_all, feature_width)
    arrived_ids = arrived_ids.reshape(slots_all, per_owner)
    doc_unit = unit_rows(doc_table)
    block_scores = lax.dot_general(
        arrived, doc_unit, (((1,), (1,)), ((), ())), preferred_element_type=jnp.float32
    )
    scores_out = jnp.take_along_axis(block_scores, arrived_ids, axis=1) * score_scale
    returned = lax.all_to_all(
        lax.all_to_all(
            scores_out.reshape(doc_groups, rep_groups, capacity, per_owner).astype(jnp.bfloat16),
            "docs",
            split_axis=0,
            concat_axis=0,
            tiled=True,
        ),
        "rep",
        split_axis=1,
        concat_axis=1,
        tiled=True,
    ).astype(jnp.float32)
    scores = returned.reshape(slots_all, per_owner)[placed]
    raised = jnp.exp(scores)
    norm_total = jnp.sum(raised, axis=(1, 2))
    label_weight = jnp.exp(labels.astype(jnp.float32))
    target = label_weight / jnp.sum(label_weight, axis=(1, 2), keepdims=True)
    losses = jnp.log(norm_total) - jnp.sum(target * scores, axis=(1, 2))
    weights = (LOSS_SCALE * (raised / norm_total[:, None, None] - target)).astype(jnp.bfloat16)
    weight_slots = (
        jnp.zeros((slots_all, per_owner), jnp.bfloat16)
        .at[target_slot]
        .set(weights.reshape(-1, per_owner))
    )
    weights_in = lax.all_to_all(
        lax.all_to_all(
            weight_slots.reshape(doc_groups, rep_groups, capacity, per_owner),
            "docs",
            split_axis=0,
            concat_axis=0,
            tiled=True,
        ),
        "rep",
        split_axis=1,
        concat_axis=1,
        tiled=True,
    )
    weights_in = weights_in.reshape(slots_all, per_owner)
    spread = (
        jnp.zeros((slots_all, doc_count), jnp.bfloat16)
        .at[jnp.arange(slots_all)[:, None], arrived_ids]
        .set(weights_in)
    )
    pull_out = (jnp.dot(spread, doc_unit, preferred_element_type=jnp.float32) * score_scale).astype(
        jnp.bfloat16
    )
    pull_out = pull_out.reshape(doc_groups, rep_groups, capacity, feature_width)
    pull_back = lax.all_to_all(
        lax.all_to_all(pull_out, "docs", split_axis=0, concat_axis=0, tiled=True),
        "rep",
        split_axis=1,
        concat_axis=1,
        tiled=True,
    )
    pull_rows = pull_back.reshape(slots_all, feature_width)[placed]
    pull_total = jnp.sum(pull_rows.astype(jnp.float32), axis=1)
    projection = jnp.mean(unit_exact * pull_total, axis=-1, keepdims=True)
    adapted_grad = ((pull_total - unit_exact * projection) / radius).astype(jnp.bfloat16)
    query_grads = lax.dot_general(
        adapted_grad, adapter, (((1,), (1,)), ((), ())), preferred_element_type=jnp.float32
    ).astype(jnp.bfloat16)
    inverse_root = 1.0 / math.sqrt(query_rows * devices)
    local_terms = lax.dot_general(
        queries, adapted_grad, (((0,), (0,)), ((), ())), preferred_element_type=jnp.float32
    )
    group_terms = lax.psum(local_terms.astype(jnp.bfloat16), "rep").astype(jnp.float32)
    summed = lax.psum_scatter(group_terms, "docs", scatter_dimension=0, tiled=True)
    adapter_grad = (summed * inverse_root).astype(jnp.bfloat16)
    return (losses, query_grads, adapter_grad)


def dot_nt(a, b):
    return lax.dot_general(a, b, (((1,), (1,)), ((), ())), preferred_element_type=jnp.float32)


def ring_group(position, groups):
    column = position // (groups // 2)
    along = position + column * (groups - 1 - 2 * position)
    return 2 * along + column


def gathered_kernel(
    groups, reps, fanout, per_owner, inverse_root,
    queries_ref, adapter_hbm, doc_hbm, meta_hbm,
    loss_ref, query_grad_ref, adapter_grad_ref,
    adapter_ref, doc_ref, docs_all, unit_all, raw_all, meta_all, radius_all,
    marks_all, here_ref, raw_turned, score_ref, weight_ref, sums, label_sum, stats, stats_in,
    pair_out, pair_in, cross_out, cross_in, near_out, near_in, pull_ref,
    grad_cols, grad_home,
    terms_out, terms_in, final_cols,
    load_sem, ring_send, ring_recv, rep_send, rep_recv, pull_send, pull_recv,
    terms_send, terms_recv, final_send, final_recv,
):
    docs_at = lax.axis_index("docs")
    rep_at = lax.axis_index("rep")
    rows, width = queries_ref.shape
    doc_count = doc_ref.shape[0]
    half = doc_count // 2
    others = reps - 1
    candidates = fanout * per_owner
    score_scale = 2.0 / math.sqrt(width)
    pull_scale = LOSS_SCALE * score_scale
    block = width // reps
    all_rows = reps * rows

    loads = [
        pltpu.make_async_copy(source, landing, load_sem.at[at])
        for at, (source, landing) in enumerate(
            (
                (doc_hbm, doc_ref),
                (queries_ref, raw_all.at[rep_at]),
                (adapter_hbm, adapter_ref),
                (meta_hbm, meta_all.at[rep_at]),
            )
        )
    ]
    for load in loads:
        load.start()

    def rep_peer(step):
        return lax.rem(rep_at + step, reps)

    pair = rep_at + 1 - 2 * lax.rem(rep_at, 2)
    cross = rep_peer(2)
    pair_cross = lax.rem(pair + 2, reps)

    along, column = docs_at // 2, docs_at % 2
    place = along + column * (groups - 1 - 2 * along)
    right = ring_group(lax.rem(place + 1, groups), groups)
    left = ring_group(lax.rem(place + groups - 1, groups), groups)

    barrier = pltpu.get_barrier_semaphore()
    for step in range(1, reps):
        pl.semaphore_signal(
            barrier, inc=1, device_id=(docs_at, rep_peer(step)), device_id_type=MESH
        )
    for step in range(1, groups):
        pl.semaphore_signal(
            barrier, inc=1, device_id=(lax.rem(docs_at + step, groups), rep_at), device_id_type=MESH
        )
    loads[0].wait()
    docs_all[0] = unit_rows(doc_ref[...])
    pl.semaphore_wait(barrier, others + groups - 1)

    def ring_copy(way, index):
        hop = index // 2
        if way == 0:
            part, source, landing, device = index % 2, hop, hop + 1, right
        else:
            part, source, landing, device = (
                1 - index % 2, (groups - hop) % groups, groups - hop - 1, left
            )
        return pltpu.make_async_remote_copy(
            src_ref=docs_all.at[source, pl.ds(part * half, half)],
            dst_ref=docs_all.at[landing, pl.ds(part * half, half)],
            send_sem=ring_send.at[way, index],
            recv_sem=ring_recv.at[way, index],
            device_id=(device, rep_at),
            device_id_type=MESH,
        )

    ring_steps = groups - 1
    for index in range(2):
        for way in range(2):
            ring_copy(way, index).start()

    def rep_copies(kind, source, landing):
        return [
            pltpu.make_async_remote_copy(
                src_ref=source(rep_peer(at + 1)),
                dst_ref=landing(at),
                send_sem=rep_send.at[kind, at],
                recv_sem=rep_recv.at[kind, at],
                device_id=(docs_at, rep_peer(at + 1)),
                device_id_type=MESH,
            )
            for at in range(others)
        ]

    def own_block(ref):
        return lambda at: ref.at[rep_at]

    loads[3].wait()
    meta_copies = rep_copies(0, own_block(meta_all), own_block(meta_all))
    for copy in meta_copies:
        copy.start()
    loads[1].wait()
    loads[2].wait()
    adapted = jnp.dot(raw_all[rep_at], adapter_ref[...], preferred_element_type=jnp.float32)
    radius = jnp.sqrt(jnp.mean(adapted * adapted, axis=-1, keepdims=True) + EPSILON)
    unit_all[rep_at] = (adapted / radius).astype(jnp.bfloat16)
    radius_all[rep_at] = jnp.broadcast_to(radius, (rows, 128))
    unit_copies = rep_copies(1, own_block(unit_all), own_block(unit_all))
    radius_copies = rep_copies(2, own_block(radius_all), own_block(radius_all))
    raw_copies = rep_copies(3, own_block(raw_all), own_block(raw_all))
    for copy in unit_copies:
        copy.start()
    stats[...] = jnp.zeros_like(stats)
    here_ref[...] = (
        lax.broadcasted_iota(jnp.int32, (doc_count, rows), 0).astype(jnp.float32).astype(jnp.bfloat16)
    )

    tile = 64
    tiles = doc_count // tile

    def label_mask(slot):
        owner = (
            ring_group(lax.rem(place + groups - slot, groups), groups) * reps + rep_at
        ).astype(jnp.float32)

        def step(index, carry):
            at = index // tiles
            first = pl.multiple_of((index % tiles) * tile, tile)
            lanes = pl.ds(pl.multiple_of(at * rows, rows), rows)
            owners = meta_all[at, 2 * candidates : 2 * candidates + 16, :].astype(jnp.float32)
            ids = jnp.full((per_owner, rows), -1.0, jnp.float32)
            marks = jnp.zeros((per_owner, rows), jnp.float32)
            for k in range(fanout):
                named = owners[k : k + 1, :] == owner
                low = k * per_owner
                ids = jnp.where(
                    named, meta_all[at, low : low + per_owner, :].astype(jnp.float32), ids
                )
                low = candidates + k * per_owner
                marks = jnp.where(
                    named, meta_all[at, low : low + per_owner, :].astype(jnp.float32) + 1.0, marks
                )
            ids = ids.astype(jnp.bfloat16)
            marks = marks.astype(jnp.bfloat16)
            here = here_ref[pl.ds(first, tile), :]
            found = jnp.zeros((tile, rows), jnp.bfloat16)
            for m in range(per_owner):
                found = jnp.where(here == ids[m : m + 1, :], marks[m : m + 1, :], found)
            marks_all[slot, pl.ds(first, tile), lanes] = found
            return carry

        lax.fori_loop(0, reps * tiles, step, 0)

    def score(slot, buffer):
        score_ref[...] = (
            dot_nt(docs_all[slot], unit_all[...].reshape(all_rows, width)) * score_scale
        )
        for at in range(reps):
            lanes = pl.ds(at * rows, rows)

            def step(index, totals):
                span = pl.ds(pl.multiple_of(index * tile, tile), tile)
                marks = marks_all[slot, span, lanes].astype(jnp.float32)
                scores = score_ref[span, lanes]
                held = marks > 0.5
                raised = jnp.where(held, jnp.exp(scores), 0.0)
                target = jnp.where(held, jnp.exp(marks - 1.0), 0.0) * label_sum[at, 0:1, :]
                weight_ref[buffer, 0, span, lanes] = raised.astype(jnp.bfloat16)
                weight_ref[buffer, 1, span, lanes] = (target * pull_scale).astype(jnp.bfloat16)
                return (
                    totals[0] + jnp.sum(raised, axis=0, keepdims=True),
                    totals[1] + jnp.sum(target * scores, axis=0, keepdims=True),
                    totals[2] + jnp.sum(raised * scores, axis=0, keepdims=True),
                )

            zero = jnp.zeros((1, rows), jnp.float32)
            norm, dotted, spread = lax.fori_loop(0, tiles, step, (zero, zero, zero))
            stats[at, 0:1, :] += norm
            stats[at, 1:2, :] += dotted
            stats[at, 2:3, :] += spread

    def accumulate(slots, first):
        for kind in range(2):
            turned = [weight_ref[buffer, kind].T for buffer in range(len(slots))]
            for at in range(reps):
                terms = [
                    jnp.dot(
                        part,
                        docs_all[slot, :, at * block : (at + 1) * block],
                        preferred_element_type=jnp.float32,
                    )
                    for part, slot in zip(turned, slots)
                ]
                if first:
                    sums[at, kind] = sum(terms)
                else:
                    sums[at, kind] += sum(terms)

    def between(index, way):
        if index == 0 and way == 0:
            for copy in meta_copies:
                copy.wait_recv()
            for at in range(reps):
                raised_labels = jnp.exp(
                    meta_all[at, candidates : 2 * candidates, :].astype(jnp.float32)
                )
                label_sum[at, 0:1, :] = 1.0 / jnp.sum(raised_labels, axis=0, keepdims=True)
        if index < 2:
            share = groups // 4
            first = (2 * index + way) * share
            for slot in range(first, first + share):
                label_mask(slot)
        elif index == 2 and way == 0:
            for copy in unit_copies:
                copy.wait_recv()
            for copy in raw_copies + radius_copies:
                copy.start()
            score(0, 0)
            accumulate((0,), True)
        elif index == 2:
            score(1, 0)
        elif index == 3 and way == 0:
            score(groups - 1, 1)
            accumulate((1, groups - 1), False)
        elif index % 2 == 0 and way == 0 and index < ring_steps - 1:
            score(index // 2, 0)
        elif index % 2 == 0 and index < ring_steps - 1:
            score(groups - index // 2, 1)
            accumulate((index // 2, groups - index // 2), False)
        elif index == ring_steps - 2 and way == 0:
            score(groups // 2 - 1, 0)
        elif index == ring_steps - 2:
            score(groups // 2 + 1, 1)
            accumulate((groups // 2 - 1, groups // 2 + 1), False)
            for copy in raw_copies:
                copy.wait_recv()
            for at in range(reps):
                raw_turned[:, at * rows : (at + 1) * rows] = raw_all[at].T

    for index in range(ring_steps):
        for way in range(2):
            ring_copy(way, index).wait_recv()
            if index + 2 < ring_steps:
                ring_copy(way, index + 2).start()
            between(index, way)
    score(groups // 2, 0)
    stat_copies = rep_copies(4, lambda at: stats, lambda at: stats_in.at[at])
    for copy in stat_copies:
        copy.start()
    last_turned = [weight_ref[0, kind].T for kind in range(2)]

    def accumulate_last(at):
        span = pl.ds(pl.multiple_of(at * block, block), block)
        for kind in range(2):
            sums[at, kind] += jnp.dot(
                last_turned[kind], docs_all[groups // 2, :, span], preferred_element_type=jnp.float32
            )

    accumulate_last(pair_cross)

    def pull_copy(at, source, landing, peer):
        return pltpu.make_async_remote_copy(
            src_ref=source,
            dst_ref=landing,
            send_sem=pull_send.at[at],
            recv_sem=pull_recv.at[at],
            device_id=(docs_at, peer),
            device_id_type=MESH,
        )

    pair_out[...] = sums[pair_cross].astype(jnp.bfloat16)
    pair_copy = pull_copy(0, pair_out, pair_in, pair)
    pair_copy.start()
    for at in (cross, pair, rep_at):
        accumulate_last(at)
    for copy in stat_copies:
        copy.wait_recv()
    shares, projections = [], []
    for at in range(reps):
        total = stats[at]
        for origin in range(others):
            total = total + stats_in[origin, at]
        stats_in[0, at] = total
        shares.append((pull_scale / total).T[:, 0:1])
        projected = (total[2:3, :] / total[0:1, :] - total[1:2, :]) * (LOSS_SCALE / width)
        projections.append(jnp.broadcast_to(projected, total.shape).T[:, 0:1])
    own_stats = stats_in[0, rep_at]
    loss_ref[...] = jnp.log(own_stats[0:1, :]) - own_stats[1:2, :]
    pair_copy.wait_recv()
    cross_copies = []
    for at in range(reps):
        span = pl.ds(at * rows, rows)
        raised = sums[cross, 0, span, :] + pair_in[0, span, :].astype(jnp.float32)
        target = sums[cross, 1, span, :] + pair_in[1, span, :].astype(jnp.float32)
        cross_out[at] = (raised * shares[at] - target).astype(jnp.bfloat16)
        copy = pull_copy(2 + at, cross_out.at[at], cross_in.at[at], cross)
        copy.start()
        cross_copies.append(copy)
    for at in range(reps):
        span = pl.ds(at * rows, rows)
        near_out[at] = (sums[pair, 0, span, :] * shares[at] - sums[pair, 1, span, :]).astype(
            jnp.bfloat16
        )
    near_copy = pull_copy(1, near_out, near_in, pair)
    near_copy.start()
    for at in range(reps):
        span = pl.ds(at * rows, rows)
        pull_ref[at] = sums[rep_at, 0, span, :] * shares[at] - sums[rep_at, 1, span, :]
    near_copy.wait_recv()
    for copy in radius_copies:
        copy.wait_recv()
    own_cols = pl.ds(pl.multiple_of(rep_at * block, block), block)
    group_terms = None
    for at in range(reps):
        held = pull_ref[at] + near_in[at].astype(jnp.float32)
        unit = unit_all[at, :, own_cols].astype(jnp.float32)
        cross_copies[at].wait_recv()
        held = held + cross_in[at].astype(jnp.float32)
        grad_cols[at] = ((held - unit * projections[at]) / radius_all[at, :, 0:1]).astype(
            jnp.bfloat16
        )
        if at == reps // 2 - 1:
            group_terms = jnp.dot(
                raw_turned[:, 0 : all_rows // 2],
                grad_cols[0 : reps // 2].reshape(all_rows // 2, block),
                preferred_element_type=jnp.float32,
            )
    grad_copies = rep_copies(5, lambda peer: grad_cols.at[peer], own_block(grad_home))
    for copy in grad_copies:
        copy.start()
    out_rows = width // groups
    parts = 2
    piece = block // parts
    group_terms += jnp.dot(
        raw_turned[:, all_rows // 2 :],
        grad_cols[reps // 2 :].reshape(all_rows // 2, block),
        preferred_element_type=jnp.float32,
    )
    group_terms = group_terms.astype(jnp.bfloat16).reshape(groups, out_rows, block)
    for part in range(parts):
        terms_out[part] = group_terms[:, :, part * piece : (part + 1) * piece]
    far_first = sorted(range(1, groups), key=lambda step: abs(step - groups // 2))
    term_copies = []
    for part in range(parts):
        for step in far_first:
            peer = lax.rem(docs_at + step, groups)
            copy = pltpu.make_async_remote_copy(
                src_ref=terms_out.at[part, peer],
                dst_ref=terms_in.at[part, step - 1],
                send_sem=terms_send.at[part, step - 1],
                recv_sem=terms_recv.at[part, step - 1],
                device_id=(peer, rep_at),
                device_id_type=MESH,
            )
            copy.start()
            term_copies.append(copy)
    grad_home[rep_at] = grad_cols[rep_at]
    for copy in grad_copies:
        copy.wait_recv()
    query_grad = dot_nt(grad_home[0], adapter_ref[:, 0:block])
    for at in range(1, reps):
        query_grad += dot_nt(grad_home[at], adapter_ref[:, at * block : (at + 1) * block])
    query_grad_ref[...] = query_grad.astype(jnp.bfloat16)
    final_copies = []
    for part in range(parts):
        summed = terms_out[part, docs_at].astype(jnp.float32)
        for at in range(groups - 1):
            term_copies[part * (groups - 1) + at].wait_recv()
        for at in range(groups - 1):
            summed = summed + terms_in[part, at].astype(jnp.float32)
        final_cols[part, rep_at] = (summed * inverse_root).astype(jnp.bfloat16)
        for at in range(others):
            copy = pltpu.make_async_remote_copy(
                src_ref=final_cols.at[part, rep_at],
                dst_ref=final_cols.at[part, rep_at],
                send_sem=final_send.at[part, at],
                recv_sem=final_recv.at[part, at],
                device_id=(docs_at, rep_peer(at + 1)),
                device_id_type=MESH,
            )
            copy.start()
            final_copies.append(copy)
    for part in range(parts):
        for at in range(others):
            final_copies[part * others + at].wait_recv()
        for at in range(reps):
            low = at * block + part * piece
            adapter_grad_ref[:, low : low + piece] = final_cols[part, at]

    for index in range(ring_steps):
        for way in range(2):
            ring_copy(way, index).wait_send()
    for copy in (
        meta_copies + unit_copies + radius_copies + raw_copies + stat_copies
        + [pair_copy, near_copy] + cross_copies + grad_copies
        + term_copies + final_copies
    ):
        copy.wait_send()


def gathered_on_device(queries, adapter, doc_table, routes, doc_rows, labels):
    groups = lax.axis_size("docs")
    reps = lax.axis_size("rep")
    rows, width = queries.shape
    fanout = routes.shape[1]
    per_owner = doc_rows.shape[2]
    doc_count = doc_table.shape[0]
    candidates = fanout * per_owner
    block = width // reps
    out_rows = width // groups
    others = reps - 1
    all_rows = reps * rows
    meta = jnp.concatenate(
        [
            doc_rows.reshape(rows, candidates),
            labels.reshape(rows, candidates),
            routes,
            jnp.zeros((rows, 16 - fanout), jnp.int32),
        ],
        axis=1,
    ).T.astype(jnp.bfloat16)
    bf16, f32 = jnp.bfloat16, jnp.float32
    vmem = pltpu.VMEM
    dma = pltpu.SemaphoreType.DMA
    losses, query_grads, adapter_grad = pl.pallas_call(
        functools.partial(
            gathered_kernel, groups, reps, fanout, per_owner,
            1.0 / math.sqrt(rows * groups * reps),
        ),
        out_shape=(
            jax.ShapeDtypeStruct((1, rows), f32),
            jax.ShapeDtypeStruct((rows, width), bf16),
            jax.ShapeDtypeStruct((out_rows, width), bf16),
        ),
        in_specs=[pl.BlockSpec(memory_space=pl.ANY)] * 4,
        out_specs=[pl.BlockSpec(memory_space=vmem)] * 3,
        scratch_shapes=[
            vmem((width, width), bf16),
            vmem((doc_count, width), bf16),
            vmem((groups, doc_count, width), bf16),
            vmem((reps, rows, width), bf16),
            vmem((reps, rows, width), bf16),
            vmem((reps, 2 * candidates + 16, rows), bf16),
            vmem((reps, rows, 128), f32),
            vmem((groups, doc_count, all_rows), bf16),
            vmem((doc_count, rows), bf16),
            vmem((width, all_rows), bf16),
            vmem((doc_count, all_rows), f32),
            vmem((2, 2, doc_count, all_rows), bf16),
            vmem((reps, 2, all_rows, block), f32),
            vmem((reps, 8, rows), f32),
            vmem((reps, 8, rows), f32),
            vmem((others, reps, 8, rows), f32),
            vmem((2, all_rows, block), bf16),
            vmem((2, all_rows, block), bf16),
            vmem((reps, rows, block), bf16),
            vmem((reps, rows, block), bf16),
            vmem((reps, rows, block), bf16),
            vmem((reps, rows, block), bf16),
            vmem((reps, rows, block), f32),
            vmem((reps, rows, block), bf16),
            vmem((reps, rows, block), bf16),
            vmem((2, groups, out_rows, block // 2), bf16),
            vmem((2, groups - 1, out_rows, block // 2), bf16),
            vmem((2, reps, out_rows, block // 2), bf16),
            dma((4,)),
            dma((2, groups - 1)),
            dma((2, groups - 1)),
            dma((6, others)),
            dma((6, others)),
            dma((2 + reps,)),
            dma((2 + reps,)),
            dma((2, groups - 1)),
            dma((2, groups - 1)),
            dma((2, others)),
            dma((2, others)),
        ],
        compiler_params=pltpu.CompilerParams(
            collective_id=0, has_side_effects=True, vmem_limit_bytes=213 * 256 * 1024
        ),
    )(
        queries, adapter, doc_table, meta,
    )
    return (losses.reshape(rows), query_grads, adapter_grad)


def on_device(queries, adapter, doc_table, routes, doc_rows, labels):
    gathered_bytes = lax.axis_size("docs") * doc_table.size * doc_table.dtype.itemsize
    if gathered_bytes <= GATHER_LIMIT and lax.axis_size("rep") == 4:
        return gathered_on_device(queries, adapter, doc_table, routes, doc_rows, labels)
    return routed_on_device(queries, adapter, doc_table, routes, doc_rows, labels)


def solution(mesh):
    placed = (
        P(("docs", "rep"), None),
        P(),
        P(("docs", "rep"), None),
        P(("docs", "rep"), None),
        P(("docs", "rep"), None, None),
        P(("docs", "rep"), None, None),
    )
    return jax.shard_map(
        on_device,
        mesh=mesh,
        in_specs=placed,
        out_specs=(P(("docs", "rep")), P(("docs", "rep"), None), P("docs", None)),
        check_vma=False,
    )
```

```python
import functools
import math

import jax
import jax.numpy as jnp
from jax import lax
from jax.experimental import pallas as pl
from jax.experimental.pallas import tpu as pltpu
from jax.sharding import PartitionSpec as P

EPSILON = 1e-06
LOSS_SCALE = 128.0
MESH = pl.DeviceIdType.MESH
GATHER_LIMIT = 8 * 1024 * 1024


def unit_rows(rows):
    widened = rows.astype(jnp.float32)
    return (
        widened / jnp.sqrt(jnp.mean(widened * widened, axis=-1, keepdims=True) + EPSILON)
    ).astype(jnp.bfloat16)


def routed_on_device(queries, adapter, doc_table, routes, doc_rows, labels):
    doc_groups = lax.axis_size("docs")
    rep_groups = lax.axis_size("rep")
    devices = doc_groups * rep_groups
    query_rows, feature_width = queries.shape
    fanout = routes.shape[1]
    per_owner = doc_rows.shape[2]
    doc_count = doc_table.shape[0]
    capacity = max(2, 2 * query_rows * fanout // devices)
    slots_all = devices * capacity
    score_scale = 2.0 / math.sqrt(feature_width)
    adapted = jnp.dot(queries, adapter, preferred_element_type=jnp.float32)
    radius = jnp.sqrt(jnp.mean(adapted * adapted, axis=-1, keepdims=True) + EPSILON)
    unit_exact = adapted / radius
    unit_query = unit_exact.astype(jnp.bfloat16)
    owner_hits = (routes[:, :, None] == jnp.arange(devices, dtype=jnp.int32)[None, None, :]).astype(
        jnp.int32
    )
    per_query = jnp.sum(owner_hits, axis=1)
    row_index = jnp.arange(query_rows, dtype=jnp.int32)
    lower_table = (row_index[:, None] > row_index[None, :]).astype(jnp.float32)
    earlier = jnp.dot(
        lower_table, per_query.astype(jnp.float32), precision=lax.Precision.HIGHEST
    ).astype(jnp.int32)
    slot_index = jnp.sum(earlier[:, None, :] * owner_hits, axis=-1)
    placed = routes * capacity + slot_index
    target_slot = placed.reshape(-1)
    repeated = jnp.broadcast_to(
        unit_query[:, None, :], (query_rows, fanout, feature_width)
    ).reshape(-1, feature_width)
    outgoing = jnp.zeros((slots_all, feature_width), jnp.bfloat16).at[target_slot].set(repeated)
    outgoing_ids = (
        jnp.zeros((slots_all, per_owner), jnp.int32)
        .at[target_slot]
        .set(doc_rows.reshape(-1, per_owner))
    )
    outgoing = outgoing.reshape(doc_groups, rep_groups, capacity, feature_width)
    outgoing_ids = outgoing_ids.reshape(doc_groups, rep_groups, capacity, per_owner)
    arrived, arrived_ids = (
        lax.all_to_all(
            lax.all_to_all(outgoing, "docs", split_axis=0, concat_axis=0, tiled=True),
            "rep",
            split_axis=1,
            concat_axis=1,
            tiled=True,
        ),
        lax.all_to_all(
            lax.all_to_all(outgoing_ids, "docs", split_axis=0, concat_axis=0, tiled=True),
            "rep",
            split_axis=1,
            concat_axis=1,
            tiled=True,
        ),
    )
    arrived = arrived.reshape(slots_all, feature_width)
    arrived_ids = arrived_ids.reshape(slots_all, per_owner)
    doc_unit = unit_rows(doc_table)
    block_scores = lax.dot_general(
        arrived, doc_unit, (((1,), (1,)), ((), ())), preferred_element_type=jnp.float32
    )
    scores_out = jnp.take_along_axis(block_scores, arrived_ids, axis=1) * score_scale
    returned = lax.all_to_all(
        lax.all_to_all(
            scores_out.reshape(doc_groups, rep_groups, capacity, per_owner).astype(jnp.bfloat16),
            "docs",
            split_axis=0,
            concat_axis=0,
            tiled=True,
        ),
        "rep",
        split_axis=1,
        concat_axis=1,
        tiled=True,
    ).astype(jnp.float32)
    scores = returned.reshape(slots_all, per_owner)[placed]
    raised = jnp.exp(scores)
    norm_total = jnp.sum(raised, axis=(1, 2))
    label_weight = jnp.exp(labels.astype(jnp.float32))
    target = label_weight / jnp.sum(label_weight, axis=(1, 2), keepdims=True)
    losses = jnp.log(norm_total) - jnp.sum(target * scores, axis=(1, 2))
    weights = (LOSS_SCALE * (raised / norm_total[:, None, None] - target)).astype(jnp.bfloat16)
    weight_slots = (
        jnp.zeros((slots_all, per_owner), jnp.bfloat16)
        .at[target_slot]
        .set(weights.reshape(-1, per_owner))
    )
    weights_in = lax.all_to_all(
        lax.all_to_all(
            weight_slots.reshape(doc_groups, rep_groups, capacity, per_owner),
            "docs",
            split_axis=0,
            concat_axis=0,
            tiled=True,
        ),
        "rep",
        split_axis=1,
        concat_axis=1,
        tiled=True,
    )
    weights_in = weights_in.reshape(slots_all, per_owner)
    spread = (
        jnp.zeros((slots_all, doc_count), jnp.bfloat16)
        .at[jnp.arange(slots_all)[:, None], arrived_ids]
        .set(weights_in)
    )
    pull_out = (jnp.dot(spread, doc_unit, preferred_element_type=jnp.float32) * score_scale).astype(
        jnp.bfloat16
    )
    pull_out = pull_out.reshape(doc_groups, rep_groups, capacity, feature_width)
    pull_back = lax.all_to_all(
        lax.all_to_all(pull_out, "docs", split_axis=0, concat_axis=0, tiled=True),
        "rep",
        split_axis=1,
        concat_axis=1,
        tiled=True,
    )
    pull_rows = pull_back.reshape(slots_all, feature_width)[placed]
    pull_total = jnp.sum(pull_rows.astype(jnp.float32), axis=1)
    projection = jnp.mean(unit_exact * pull_total, axis=-1, keepdims=True)
    adapted_grad = ((pull_total - unit_exact * projection) / radius).astype(jnp.bfloat16)
    query_grads = lax.dot_general(
        adapted_grad, adapter, (((1,), (1,)), ((), ())), preferred_element_type=jnp.float32
    ).astype(jnp.bfloat16)
    inverse_root = 1.0 / math.sqrt(query_rows * devices)
    local_terms = lax.dot_general(
        queries, adapted_grad, (((0,), (0,)), ((), ())), preferred_element_type=jnp.float32
    )
    group_terms = lax.psum(local_terms.astype(jnp.bfloat16), "rep").astype(jnp.float32)
    summed = lax.psum_scatter(group_terms, "docs", scatter_dimension=0, tiled=True)
    adapter_grad = (summed * inverse_root).astype(jnp.bfloat16)
    return (losses, query_grads, adapter_grad)


def dot_nt(a, b):
    return lax.dot_general(a, b, (((1,), (1,)), ((), ())), preferred_element_type=jnp.float32)


def ring_group(position, groups):
    column = position // (groups // 2)
    along = position + column * (groups - 1 - 2 * position)
    return 2 * along + column


def gathered_kernel(
    groups, reps, fanout, per_owner, inverse_root,
    queries_ref, adapter_hbm, doc_hbm, meta_hbm,
    loss_ref, query_grad_ref, adapter_grad_ref,
    adapter_ref, doc_ref, docs_all, unit_all, raw_all, meta_ref, meta_all, radius_all,
    marks_all, here_ref, raw_turned, score_ref, weight_ref, sums, label_sum, stats, stats_in,
    pair_out, pair_in, cross_out, cross_in, near_out, near_in, pull_ref,
    grad_cols, grad_home,
    terms_out, travel_out, travel_in, final_cols,
    load_sem, ring_send, ring_recv, rep_send, rep_recv, pull_send, pull_recv,
    terms_send, terms_recv, final_send, final_recv,
):
    docs_at = lax.axis_index("docs")
    rep_at = lax.axis_index("rep")
    rows, width = queries_ref.shape
    doc_count = doc_ref.shape[0]
    half = doc_count // 2
    others = reps - 1
    candidates = fanout * per_owner
    score_scale = 2.0 / math.sqrt(width)
    pull_scale = LOSS_SCALE * score_scale
    block = width // reps
    all_rows = reps * rows

    loads = [
        pltpu.make_async_copy(source, landing, load_sem.at[at])
        for at, (source, landing) in enumerate(
            (
                (doc_hbm, doc_ref),
                (queries_ref, raw_all.at[rep_at]),
                (adapter_hbm, adapter_ref),
                (meta_hbm, meta_ref),
            )
        )
    ]
    for load in loads:
        load.start()

    def rep_peer(step):
        return lax.rem(rep_at + step, reps)

    pair = rep_at + 1 - 2 * lax.rem(rep_at, 2)
    cross = rep_peer(2)
    pair_cross = lax.rem(pair + 2, reps)

    along, column = docs_at // 2, docs_at % 2
    place = along + column * (groups - 1 - 2 * along)
    right = ring_group(lax.rem(place + 1, groups), groups)
    left = ring_group(lax.rem(place + groups - 1, groups), groups)

    barrier = pltpu.get_barrier_semaphore()
    for step in range(1, reps):
        pl.semaphore_signal(
            barrier, inc=1, device_id=(docs_at, rep_peer(step)), device_id_type=MESH
        )
    for step in range(1, groups):
        pl.semaphore_signal(
            barrier, inc=1, device_id=(lax.rem(docs_at + step, groups), rep_at), device_id_type=MESH
        )
    loads[0].wait()
    docs_all[0] = unit_rows(doc_ref[...])
    pl.semaphore_wait(barrier, others + groups - 1)

    def ring_copy(way, index):
        hop = index // 2
        if way == 0:
            part, source, landing, device = index % 2, hop, hop + 1, right
        else:
            part, source, landing, device = (
                1 - index % 2, (groups - hop) % groups, groups - hop - 1, left
            )
        return pltpu.make_async_remote_copy(
            src_ref=docs_all.at[source, pl.ds(part * half, half)],
            dst_ref=docs_all.at[landing, pl.ds(part * half, half)],
            send_sem=ring_send.at[way, index],
            recv_sem=ring_recv.at[way, index],
            device_id=(device, rep_at),
            device_id_type=MESH,
        )

    ring_steps = groups - 1
    for index in range(2):
        for way in range(2):
            ring_copy(way, index).start()

    def rep_copies(kind, source, landing):
        return [
            pltpu.make_async_remote_copy(
                src_ref=source(rep_peer(at + 1)),
                dst_ref=landing(at),
                send_sem=rep_send.at[kind, at],
                recv_sem=rep_recv.at[kind, at],
                device_id=(docs_at, rep_peer(at + 1)),
                device_id_type=MESH,
            )
            for at in range(others)
        ]

    def own_block(ref):
        return lambda at: ref.at[rep_at]

    loads[3].wait()
    meta_all[rep_at] = meta_ref[...].astype(jnp.float32).astype(jnp.bfloat16)
    meta_copies = rep_copies(0, own_block(meta_all), own_block(meta_all))
    for copy in meta_copies:
        copy.start()
    loads[1].wait()
    loads[2].wait()
    adapted = jnp.dot(raw_all[rep_at], adapter_ref[...], preferred_element_type=jnp.float32)
    radius = jnp.sqrt(jnp.mean(adapted * adapted, axis=-1, keepdims=True) + EPSILON)
    unit_all[rep_at] = (adapted / radius).astype(jnp.bfloat16)
    radius_all[rep_at] = jnp.broadcast_to(radius, (rows, 128))
    unit_copies = rep_copies(1, own_block(unit_all), own_block(unit_all))
    radius_copies = rep_copies(2, own_block(radius_all), own_block(radius_all))
    raw_copies = rep_copies(3, own_block(raw_all), own_block(raw_all))
    for copy in unit_copies:
        copy.start()
    stats[...] = jnp.zeros_like(stats)
    here_ref[...] = (
        lax.broadcasted_iota(jnp.int32, (doc_count, rows), 0).astype(jnp.float32).astype(jnp.bfloat16)
    )

    tile = 64
    tiles = doc_count // tile

    def label_mask(slot):
        owner = (
            ring_group(lax.rem(place + groups - slot, groups), groups) * reps + rep_at
        ).astype(jnp.float32)

        def step(index, carry):
            at = index // tiles
            first = pl.multiple_of((index % tiles) * tile, tile)
            lanes = pl.ds(pl.multiple_of(at * rows, rows), rows)
            owners = meta_all[at, 2 * candidates : 2 * candidates + 16, :].astype(jnp.float32)
            ids = jnp.full((per_owner, rows), -1.0, jnp.float32)
            marks = jnp.zeros((per_owner, rows), jnp.float32)
            for k in range(fanout):
                named = owners[k : k + 1, :] == owner
                low = k * per_owner
                ids = jnp.where(
                    named, meta_all[at, low : low + per_owner, :].astype(jnp.float32), ids
                )
                low = candidates + k * per_owner
                marks = jnp.where(
                    named, meta_all[at, low : low + per_owner, :].astype(jnp.float32) + 1.0, marks
                )
            ids = ids.astype(jnp.bfloat16)
            marks = marks.astype(jnp.bfloat16)
            here = here_ref[pl.ds(first, tile), :]
            found = jnp.zeros((tile, rows), jnp.bfloat16)
            for m in range(per_owner):
                found = jnp.where(here == ids[m : m + 1, :], marks[m : m + 1, :], found)
            marks_all[slot, pl.ds(first, tile), lanes] = found
            return carry

        lax.fori_loop(0, reps * tiles, step, 0)

    def score(slot, buffer):
        score_ref[...] = (
            dot_nt(docs_all[slot], unit_all[...].reshape(all_rows, width)) * score_scale
        )
        for at in range(reps):
            lanes = pl.ds(at * rows, rows)

            def step(index, totals):
                span = pl.ds(pl.multiple_of(index * tile, tile), tile)
                marks = marks_all[slot, span, lanes].astype(jnp.float32)
                scores = score_ref[span, lanes]
                held = marks > 0.5
                raised = jnp.where(held, jnp.exp(scores), 0.0)
                target = jnp.where(held, jnp.exp(marks - 1.0), 0.0) * label_sum[at, 0:1, :]
                weight_ref[buffer, 0, span, lanes] = raised.astype(jnp.bfloat16)
                weight_ref[buffer, 1, span, lanes] = (target * pull_scale).astype(jnp.bfloat16)
                return (
                    totals[0] + jnp.sum(raised, axis=0, keepdims=True),
                    totals[1] + jnp.sum(target * scores, axis=0, keepdims=True),
                    totals[2] + jnp.sum(raised * scores, axis=0, keepdims=True),
                )

            zero = jnp.zeros((1, rows), jnp.float32)
            norm, dotted, spread = lax.fori_loop(0, tiles, step, (zero, zero, zero))
            stats[at, 0:1, :] += norm
            stats[at, 1:2, :] += dotted
            stats[at, 2:3, :] += spread

    def accumulate(slots, first):
        for kind in range(2):
            turned = [weight_ref[buffer, kind].T for buffer in range(len(slots))]
            for at in range(reps):
                terms = [
                    jnp.dot(
                        part,
                        docs_all[slot, :, at * block : (at + 1) * block],
                        preferred_element_type=jnp.float32,
                    )
                    for part, slot in zip(turned, slots)
                ]
                if first:
                    sums[at, kind] = sum(terms)
                else:
                    sums[at, kind] += sum(terms)

    def between(index, way):
        if index == 0 and way == 0:
            for copy in meta_copies:
                copy.wait_recv()
            for at in range(reps):
                raised_labels = jnp.exp(
                    meta_all[at, candidates : 2 * candidates, :].astype(jnp.float32)
                )
                label_sum[at, 0:1, :] = 1.0 / jnp.sum(raised_labels, axis=0, keepdims=True)
        if index < 2:
            share = groups // 4
            first = (2 * index + way) * share
            for slot in range(first, first + share):
                label_mask(slot)
        elif index == 2 and way == 0:
            for copy in unit_copies:
                copy.wait_recv()
            for copy in raw_copies + radius_copies:
                copy.start()
            score(0, 0)
            accumulate((0,), True)
        elif index == 2:
            score(1, 0)
        elif index == 3 and way == 0:
            score(groups - 1, 1)
            accumulate((1, groups - 1), False)
        elif index % 2 == 0 and way == 0 and index < ring_steps - 1:
            score(index // 2, 0)
        elif index % 2 == 0 and index < ring_steps - 1:
            score(groups - index // 2, 1)
            accumulate((index // 2, groups - index // 2), False)
        elif index == ring_steps - 2 and way == 0:
            score(groups // 2 - 1, 0)
        elif index == ring_steps - 2:
            score(groups // 2 + 1, 1)
            accumulate((groups // 2 - 1, groups // 2 + 1), False)
            for copy in raw_copies:
                copy.wait_recv()
            for at in range(reps):
                raw_turned[:, at * rows : (at + 1) * rows] = raw_all[at].T

    for index in range(ring_steps):
        for way in range(2):
            ring_copy(way, index).wait_recv()
            if index + 2 < ring_steps:
                ring_copy(way, index + 2).start()
            between(index, way)
    score(groups // 2, 0)
    stat_copies = rep_copies(4, lambda at: stats, lambda at: stats_in.at[at])
    for copy in stat_copies:
        copy.start()
    last_turned = [weight_ref[0, kind].T for kind in range(2)]

    def accumulate_last(at):
        span = pl.ds(pl.multiple_of(at * block, block), block)
        for kind in range(2):
            sums[at, kind] += jnp.dot(
                last_turned[kind], docs_all[groups // 2, :, span], preferred_element_type=jnp.float32
            )

    accumulate_last(pair_cross)

    def pull_copy(at, source, landing, peer):
        return pltpu.make_async_remote_copy(
            src_ref=source,
            dst_ref=landing,
            send_sem=pull_send.at[at],
            recv_sem=pull_recv.at[at],
            device_id=(docs_at, peer),
            device_id_type=MESH,
        )

    pair_out[...] = sums[pair_cross].astype(jnp.bfloat16)
    pair_copy = pull_copy(0, pair_out, pair_in, pair)
    pair_copy.start()
    for at in (cross, pair, rep_at):
        accumulate_last(at)
    for copy in stat_copies:
        copy.wait_recv()
    shares, projections = [], []
    for at in range(reps):
        total = stats[at]
        for origin in range(others):
            total = total + stats_in[origin, at]
        stats_in[0, at] = total
        shares.append((pull_scale / total).T[:, 0:1])
        projected = (total[2:3, :] / total[0:1, :] - total[1:2, :]) * (LOSS_SCALE / width)
        projections.append(jnp.broadcast_to(projected, total.shape).T[:, 0:1])
    own_stats = stats_in[0, rep_at]
    loss_ref[...] = jnp.log(own_stats[0:1, :]) - own_stats[1:2, :]
    pair_copy.wait_recv()
    cross_copies = []
    for at in range(reps):
        span = pl.ds(at * rows, rows)
        raised = sums[cross, 0, span, :] + pair_in[0, span, :].astype(jnp.float32)
        target = sums[cross, 1, span, :] + pair_in[1, span, :].astype(jnp.float32)
        cross_out[at] = (raised * shares[at] - target).astype(jnp.bfloat16)
        copy = pull_copy(2 + at, cross_out.at[at], cross_in.at[at], cross)
        copy.start()
        cross_copies.append(copy)
    for at in range(reps):
        span = pl.ds(at * rows, rows)
        near_out[at] = (sums[pair, 0, span, :] * shares[at] - sums[pair, 1, span, :]).astype(
            jnp.bfloat16
        )
    near_copy = pull_copy(1, near_out, near_in, pair)
    near_copy.start()
    for at in range(reps):
        span = pl.ds(at * rows, rows)
        pull_ref[at] = sums[rep_at, 0, span, :] * shares[at] - sums[rep_at, 1, span, :]
    near_copy.wait_recv()
    for copy in radius_copies:
        copy.wait_recv()
    own_cols = pl.ds(pl.multiple_of(rep_at * block, block), block)
    group_terms = None
    for at in range(reps):
        held = pull_ref[at] + near_in[at].astype(jnp.float32)
        unit = unit_all[at, :, own_cols].astype(jnp.float32)
        cross_copies[at].wait_recv()
        held = held + cross_in[at].astype(jnp.float32)
        grad_cols[at] = ((held - unit * projections[at]) / radius_all[at, :, 0:1]).astype(
            jnp.bfloat16
        )
        if at == reps // 2 - 1:
            group_terms = jnp.dot(
                raw_turned[:, 0 : all_rows // 2],
                grad_cols[0 : reps // 2].reshape(all_rows // 2, block),
                preferred_element_type=jnp.float32,
            )
    grad_copies = rep_copies(5, lambda peer: grad_cols.at[peer], own_block(grad_home))
    for copy in grad_copies:
        copy.start()
    out_rows = width // groups
    parts = 2
    piece = block // parts
    group_terms += jnp.dot(
        raw_turned[:, all_rows // 2 :],
        grad_cols[reps // 2 :].reshape(all_rows // 2, block),
        preferred_element_type=jnp.float32,
    )
    group_terms = group_terms.astype(jnp.bfloat16).reshape(groups, out_rows, block)
    for part in range(parts):
        terms_out[part] = group_terms[:, :, part * piece : (part + 1) * piece]
    hops = groups // 2

    def term_copy(way, part, step):
        return pltpu.make_async_remote_copy(
            src_ref=travel_out.at[way, part, step],
            dst_ref=travel_in.at[way, part, step],
            send_sem=terms_send.at[way, part, step],
            recv_sem=terms_recv.at[way, part, step],
            device_id=(right if way == 0 else left, rep_at),
            device_id_type=MESH,
        )

    term_copies = []
    for step in range(hops):
        distance = hops - step
        for part, way in ((0, 0), (1, 1), (1, 0), (0, 1)):
            start = 0 if part == way else 1
            if step < start:
                continue
            ahead = distance if way == 0 else groups - distance
            target = ring_group(lax.rem(place + ahead, groups), groups)
            running = terms_out[part, target]
            if step > start:
                term_copy(way, part, step - 1).wait_recv()
                running = (
                    running.astype(jnp.float32) + travel_in[way, part, step - 1].astype(jnp.float32)
                ).astype(jnp.bfloat16)
            travel_out[way, part, step] = running
            copy = term_copy(way, part, step)
            copy.start()
            term_copies.append(copy)
        if step == hops - 2:
            grad_home[rep_at] = grad_cols[rep_at]
            for copy in grad_copies:
                copy.wait_recv()
            query_grad = dot_nt(grad_home[0], adapter_ref[:, 0:block])
            for at in range(1, reps):
                query_grad += dot_nt(grad_home[at], adapter_ref[:, at * block : (at + 1) * block])
            query_grad_ref[...] = query_grad.astype(jnp.bfloat16)
    final_copies = []
    for part in range(parts):
        summed = terms_out[part, docs_at].astype(jnp.float32)
        for way in range(2):
            term_copy(way, part, hops - 1).wait_recv()
            summed = summed + travel_in[way, part, hops - 1].astype(jnp.float32)
        final_cols[part, rep_at] = (summed * inverse_root).astype(jnp.bfloat16)
        for at in range(others):
            copy = pltpu.make_async_remote_copy(
                src_ref=final_cols.at[part, rep_at],
                dst_ref=final_cols.at[part, rep_at],
                send_sem=final_send.at[part, at],
                recv_sem=final_recv.at[part, at],
                device_id=(docs_at, rep_peer(at + 1)),
                device_id_type=MESH,
            )
            copy.start()
            final_copies.append(copy)
    for part in range(parts):
        for at in range(others):
            final_copies[part * others + at].wait_recv()
        for at in range(reps):
            low = at * block + part * piece
            adapter_grad_ref[:, low : low + piece] = final_cols[part, at]

    for index in range(ring_steps):
        for way in range(2):
            ring_copy(way, index).wait_send()
    for copy in (
        meta_copies + unit_copies + radius_copies + raw_copies + stat_copies
        + [pair_copy, near_copy] + cross_copies + grad_copies
        + term_copies + final_copies
    ):
        copy.wait_send()


def gathered_on_device(queries, adapter, doc_table, routes, doc_rows, labels):
    groups = lax.axis_size("docs")
    reps = lax.axis_size("rep")
    rows, width = queries.shape
    fanout = routes.shape[1]
    per_owner = doc_rows.shape[2]
    doc_count = doc_table.shape[0]
    candidates = fanout * per_owner
    block = width // reps
    out_rows = width // groups
    others = reps - 1
    all_rows = reps * rows
    meta = jnp.concatenate(
        [
            doc_rows.reshape(rows, candidates),
            labels.reshape(rows, candidates),
            routes,
            jnp.zeros((rows, 16 - fanout), jnp.int32),
        ],
        axis=1,
    ).T
    bf16, f32 = jnp.bfloat16, jnp.float32
    vmem = pltpu.VMEM
    dma = pltpu.SemaphoreType.DMA
    losses, query_grads, adapter_grad = pl.pallas_call(
        functools.partial(
            gathered_kernel, groups, reps, fanout, per_owner,
            1.0 / math.sqrt(rows * groups * reps),
        ),
        out_shape=(
            jax.ShapeDtypeStruct((1, rows), f32),
            jax.ShapeDtypeStruct((rows, width), bf16),
            jax.ShapeDtypeStruct((out_rows, width), bf16),
        ),
        in_specs=[pl.BlockSpec(memory_space=pl.ANY)] * 4,
        out_specs=[pl.BlockSpec(memory_space=vmem)] * 3,
        scratch_shapes=[
            vmem((width, width), bf16),
            vmem((doc_count, width), bf16),
            vmem((groups, doc_count, width), bf16),
            vmem((reps, rows, width), bf16),
            vmem((reps, rows, width), bf16),
            vmem((2 * candidates + 16, rows), jnp.int32),
            vmem((reps, 2 * candidates + 16, rows), bf16),
            vmem((reps, rows, 128), f32),
            vmem((groups, doc_count, all_rows), bf16),
            vmem((doc_count, rows), bf16),
            vmem((width, all_rows), bf16),
            vmem((doc_count, all_rows), f32),
            vmem((2, 2, doc_count, all_rows), bf16),
            vmem((reps, 2, all_rows, block), f32),
            vmem((reps, 8, rows), f32),
            vmem((reps, 8, rows), f32),
            vmem((others, reps, 8, rows), f32),
            vmem((2, all_rows, block), bf16),
            vmem((2, all_rows, block), bf16),
            vmem((reps, rows, block), bf16),
            vmem((reps, rows, block), bf16),
            vmem((reps, rows, block), bf16),
            vmem((reps, rows, block), bf16),
            vmem((reps, rows, block), f32),
            vmem((reps, rows, block), bf16),
            vmem((reps, rows, block), bf16),
            vmem((2, groups, out_rows, block // 2), bf16),
            vmem((2, 2, groups // 2, out_rows, block // 2), bf16),
            vmem((2, 2, groups // 2, out_rows, block // 2), bf16),
            vmem((2, reps, out_rows, block // 2), bf16),
            dma((4,)),
            dma((2, groups - 1)),
            dma((2, groups - 1)),
            dma((6, others)),
            dma((6, others)),
            dma((2 + reps,)),
            dma((2 + reps,)),
            dma((2, 2, groups // 2)),
            dma((2, 2, groups // 2)),
            dma((2, others)),
            dma((2, others)),
        ],
        compiler_params=pltpu.CompilerParams(
            collective_id=0, has_side_effects=True, vmem_limit_bytes=213 * 256 * 1024
        ),
    )(
        queries, adapter, doc_table, meta,
    )
    return (losses.reshape(rows), query_grads, adapter_grad)


def on_device(queries, adapter, doc_table, routes, doc_rows, labels):
    gathered_bytes = lax.axis_size("docs") * doc_table.size * doc_table.dtype.itemsize
    if gathered_bytes <= GATHER_LIMIT and lax.axis_size("rep") == 4:
        return gathered_on_device(queries, adapter, doc_table, routes, doc_rows, labels)
    return routed_on_device(queries, adapter, doc_table, routes, doc_rows, labels)


def solution(mesh):
    placed = (
        P(("docs", "rep"), None),
        P(),
        P(("docs", "rep"), None),
        P(("docs", "rep"), None),
        P(("docs", "rep"), None, None),
        P(("docs", "rep"), None, None),
    )
    return jax.shard_map(
        on_device,
        mesh=mesh,
        in_specs=placed,
        out_specs=(P(("docs", "rep")), P(("docs", "rep"), None), P("docs", None)),
        check_vma=False,
    )
```

```python
import functools
import math

import jax
import jax.numpy as jnp
from jax import lax
from jax.experimental import pallas as pl
from jax.experimental.pallas import tpu as pltpu
from jax.sharding import PartitionSpec as P

EPSILON = 1e-06
LOSS_SCALE = 128.0
MESH = pl.DeviceIdType.MESH
GATHER_LIMIT = 8 * 1024 * 1024


def unit_rows(rows):
    widened = rows.astype(jnp.float32)
    return (
        widened / jnp.sqrt(jnp.mean(widened * widened, axis=-1, keepdims=True) + EPSILON)
    ).astype(jnp.bfloat16)


def routed_on_device(queries, adapter, doc_table, routes, doc_rows, labels):
    doc_groups = lax.axis_size("docs")
    rep_groups = lax.axis_size("rep")
    devices = doc_groups * rep_groups
    query_rows, feature_width = queries.shape
    fanout = routes.shape[1]
    per_owner = doc_rows.shape[2]
    doc_count = doc_table.shape[0]
    capacity = max(2, 2 * query_rows * fanout // devices)
    slots_all = devices * capacity
    score_scale = 2.0 / math.sqrt(feature_width)
    adapted = jnp.dot(queries, adapter, preferred_element_type=jnp.float32)
    radius = jnp.sqrt(jnp.mean(adapted * adapted, axis=-1, keepdims=True) + EPSILON)
    unit_exact = adapted / radius
    unit_query = unit_exact.astype(jnp.bfloat16)
    owner_hits = (routes[:, :, None] == jnp.arange(devices, dtype=jnp.int32)[None, None, :]).astype(
        jnp.int32
    )
    per_query = jnp.sum(owner_hits, axis=1)
    row_index = jnp.arange(query_rows, dtype=jnp.int32)
    lower_table = (row_index[:, None] > row_index[None, :]).astype(jnp.float32)
    earlier = jnp.dot(
        lower_table, per_query.astype(jnp.float32), precision=lax.Precision.HIGHEST
    ).astype(jnp.int32)
    slot_index = jnp.sum(earlier[:, None, :] * owner_hits, axis=-1)
    placed = routes * capacity + slot_index
    target_slot = placed.reshape(-1)
    repeated = jnp.broadcast_to(
        unit_query[:, None, :], (query_rows, fanout, feature_width)
    ).reshape(-1, feature_width)
    outgoing = jnp.zeros((slots_all, feature_width), jnp.bfloat16).at[target_slot].set(repeated)
    outgoing_ids = (
        jnp.zeros((slots_all, per_owner), jnp.int32)
        .at[target_slot]
        .set(doc_rows.reshape(-1, per_owner))
    )
    outgoing = outgoing.reshape(doc_groups, rep_groups, capacity, feature_width)
    outgoing_ids = outgoing_ids.reshape(doc_groups, rep_groups, capacity, per_owner)
    arrived, arrived_ids = (
        lax.all_to_all(
            lax.all_to_all(outgoing, "docs", split_axis=0, concat_axis=0, tiled=True),
            "rep",
            split_axis=1,
            concat_axis=1,
            tiled=True,
        ),
        lax.all_to_all(
            lax.all_to_all(outgoing_ids, "docs", split_axis=0, concat_axis=0, tiled=True),
            "rep",
            split_axis=1,
            concat_axis=1,
            tiled=True,
        ),
    )
    arrived = arrived.reshape(slots_all, feature_width)
    arrived_ids = arrived_ids.reshape(slots_all, per_owner)
    doc_unit = unit_rows(doc_table)
    block_scores = lax.dot_general(
        arrived, doc_unit, (((1,), (1,)), ((), ())), preferred_element_type=jnp.float32
    )
    scores_out = jnp.take_along_axis(block_scores, arrived_ids, axis=1) * score_scale
    returned = lax.all_to_all(
        lax.all_to_all(
            scores_out.reshape(doc_groups, rep_groups, capacity, per_owner).astype(jnp.bfloat16),
            "docs",
            split_axis=0,
            concat_axis=0,
            tiled=True,
        ),
        "rep",
        split_axis=1,
        concat_axis=1,
        tiled=True,
    ).astype(jnp.float32)
    scores = returned.reshape(slots_all, per_owner)[placed]
    raised = jnp.exp(scores)
    norm_total = jnp.sum(raised, axis=(1, 2))
    label_weight = jnp.exp(labels.astype(jnp.float32))
    target = label_weight / jnp.sum(label_weight, axis=(1, 2), keepdims=True)
    losses = jnp.log(norm_total) - jnp.sum(target * scores, axis=(1, 2))
    weights = (LOSS_SCALE * (raised / norm_total[:, None, None] - target)).astype(jnp.bfloat16)
    weight_slots = (
        jnp.zeros((slots_all, per_owner), jnp.bfloat16)
        .at[target_slot]
        .set(weights.reshape(-1, per_owner))
    )
    weights_in = lax.all_to_all(
        lax.all_to_all(
            weight_slots.reshape(doc_groups, rep_groups, capacity, per_owner),
            "docs",
            split_axis=0,
            concat_axis=0,
            tiled=True,
        ),
        "rep",
        split_axis=1,
        concat_axis=1,
        tiled=True,
    )
    weights_in = weights_in.reshape(slots_all, per_owner)
    spread = (
        jnp.zeros((slots_all, doc_count), jnp.bfloat16)
        .at[jnp.arange(slots_all)[:, None], arrived_ids]
        .set(weights_in)
    )
    pull_out = (jnp.dot(spread, doc_unit, preferred_element_type=jnp.float32) * score_scale).astype(
        jnp.bfloat16
    )
    pull_out = pull_out.reshape(doc_groups, rep_groups, capacity, feature_width)
    pull_back = lax.all_to_all(
        lax.all_to_all(pull_out, "docs", split_axis=0, concat_axis=0, tiled=True),
        "rep",
        split_axis=1,
        concat_axis=1,
        tiled=True,
    )
    pull_rows = pull_back.reshape(slots_all, feature_width)[placed]
    pull_total = jnp.sum(pull_rows.astype(jnp.float32), axis=1)
    projection = jnp.mean(unit_exact * pull_total, axis=-1, keepdims=True)
    adapted_grad = ((pull_total - unit_exact * projection) / radius).astype(jnp.bfloat16)
    query_grads = lax.dot_general(
        adapted_grad, adapter, (((1,), (1,)), ((), ())), preferred_element_type=jnp.float32
    ).astype(jnp.bfloat16)
    inverse_root = 1.0 / math.sqrt(query_rows * devices)
    local_terms = lax.dot_general(
        queries, adapted_grad, (((0,), (0,)), ((), ())), preferred_element_type=jnp.float32
    )
    group_terms = lax.psum(local_terms.astype(jnp.bfloat16), "rep").astype(jnp.float32)
    summed = lax.psum_scatter(group_terms, "docs", scatter_dimension=0, tiled=True)
    adapter_grad = (summed * inverse_root).astype(jnp.bfloat16)
    return (losses, query_grads, adapter_grad)


def dot_nt(a, b):
    return lax.dot_general(a, b, (((1,), (1,)), ((), ())), preferred_element_type=jnp.float32)


def ring_group(position, groups):
    column = position // (groups // 2)
    along = position + column * (groups - 1 - 2 * position)
    return 2 * along + column


def gathered_kernel(
    groups, reps, fanout, per_owner, inverse_root,
    queries_ref, adapter_hbm, doc_hbm, meta_hbm,
    loss_ref, query_grad_ref, adapter_grad_ref,
    adapter_ref, doc_ref, docs_all, unit_all, raw_all, meta_ref, meta_all, radius_all,
    marks_all, here_ref, raw_turned, score_ref, weight_ref, sums, label_sum, stats, stats_in,
    pair_out, pair_in, cross_out, cross_in, near_out, near_in, pull_ref,
    grad_cols, grad_home,
    terms_out, terms_in, final_cols,
    load_sem, ring_send, ring_recv, rep_send, rep_recv, pull_send, pull_recv,
    terms_send, terms_recv, final_send, final_recv,
):
    docs_at = lax.axis_index("docs")
    rep_at = lax.axis_index("rep")
    rows, width = queries_ref.shape
    doc_count = doc_ref.shape[0]
    half = doc_count // 2
    others = reps - 1
    candidates = fanout * per_owner
    score_scale = 2.0 / math.sqrt(width)
    pull_scale = LOSS_SCALE * score_scale
    block = width // reps
    all_rows = reps * rows

    loads = [
        pltpu.make_async_copy(source, landing, load_sem.at[at])
        for at, (source, landing) in enumerate(
            (
                (doc_hbm, doc_ref),
                (queries_ref, raw_all.at[rep_at]),
                (adapter_hbm, adapter_ref),
                (meta_hbm, meta_ref),
            )
        )
    ]
    for load in loads:
        load.start()

    def rep_peer(step):
        return lax.rem(rep_at + step, reps)

    pair = rep_at + 1 - 2 * lax.rem(rep_at, 2)
    cross = rep_peer(2)
    pair_cross = lax.rem(pair + 2, reps)

    along, column = docs_at // 2, docs_at % 2
    place = along + column * (groups - 1 - 2 * along)
    right = ring_group(lax.rem(place + 1, groups), groups)
    left = ring_group(lax.rem(place + groups - 1, groups), groups)

    barrier = pltpu.get_barrier_semaphore()
    for step in range(1, reps):
        pl.semaphore_signal(
            barrier, inc=1, device_id=(docs_at, rep_peer(step)), device_id_type=MESH
        )
    for step in range(1, groups):
        pl.semaphore_signal(
            barrier, inc=1, device_id=(lax.rem(docs_at + step, groups), rep_at), device_id_type=MESH
        )
    loads[0].wait()
    docs_all[0] = unit_rows(doc_ref[...])
    pl.semaphore_wait(barrier, others + groups - 1)

    def ring_copy(way, index):
        hop = index // 2
        if way == 0:
            part, source, landing, device = index % 2, hop, hop + 1, right
        else:
            part, source, landing, device = (
                1 - index % 2, (groups - hop) % groups, groups - hop - 1, left
            )
        return pltpu.make_async_remote_copy(
            src_ref=docs_all.at[source, pl.ds(part * half, half)],
            dst_ref=docs_all.at[landing, pl.ds(part * half, half)],
            send_sem=ring_send.at[way, index],
            recv_sem=ring_recv.at[way, index],
            device_id=(device, rep_at),
            device_id_type=MESH,
        )

    ring_steps = groups - 1
    for index in range(2):
        for way in range(2):
            ring_copy(way, index).start()

    def rep_copies(kind, source, landing):
        return [
            pltpu.make_async_remote_copy(
                src_ref=source(rep_peer(at + 1)),
                dst_ref=landing(at),
                send_sem=rep_send.at[kind, at],
                recv_sem=rep_recv.at[kind, at],
                device_id=(docs_at, rep_peer(at + 1)),
                device_id_type=MESH,
            )
            for at in range(others)
        ]

    def own_block(ref):
        return lambda at: ref.at[rep_at]

    loads[3].wait()
    meta_all[rep_at] = meta_ref[...].astype(jnp.float32).astype(jnp.bfloat16)
    meta_copies = rep_copies(0, own_block(meta_all), own_block(meta_all))
    for copy in meta_copies:
        copy.start()
    loads[1].wait()
    loads[2].wait()
    adapted = jnp.dot(raw_all[rep_at], adapter_ref[...], preferred_element_type=jnp.float32)
    radius = jnp.sqrt(jnp.mean(adapted * adapted, axis=-1, keepdims=True) + EPSILON)
    unit_all[rep_at] = (adapted / radius).astype(jnp.bfloat16)
    radius_all[rep_at] = jnp.broadcast_to(radius, (rows, 128))
    unit_copies = rep_copies(1, own_block(unit_all), own_block(unit_all))
    radius_copies = rep_copies(2, own_block(radius_all), own_block(radius_all))
    raw_copies = rep_copies(3, own_block(raw_all), own_block(raw_all))
    for copy in unit_copies:
        copy.start()
    stats[...] = jnp.zeros_like(stats)
    here_ref[...] = (
        lax.broadcasted_iota(jnp.int32, (doc_count, rows), 0).astype(jnp.float32).astype(jnp.bfloat16)
    )

    tile = 64
    tiles = doc_count // tile

    def label_mask(slot):
        owner = (
            ring_group(lax.rem(place + groups - slot, groups), groups) * reps + rep_at
        ).astype(jnp.float32)

        def step(index, carry):
            at = index // tiles
            first = pl.multiple_of((index % tiles) * tile, tile)
            lanes = pl.ds(pl.multiple_of(at * rows, rows), rows)
            owners = meta_all[at, 2 * candidates : 2 * candidates + 16, :].astype(jnp.float32)
            ids = jnp.full((per_owner, rows), -1.0, jnp.float32)
            marks = jnp.zeros((per_owner, rows), jnp.float32)
            for k in range(fanout):
                named = owners[k : k + 1, :] == owner
                low = k * per_owner
                ids = jnp.where(
                    named, meta_all[at, low : low + per_owner, :].astype(jnp.float32), ids
                )
                low = candidates + k * per_owner
                marks = jnp.where(
                    named, meta_all[at, low : low + per_owner, :].astype(jnp.float32) + 1.0, marks
                )
            ids = ids.astype(jnp.bfloat16)
            marks = marks.astype(jnp.bfloat16)
            here = here_ref[pl.ds(first, tile), :]
            found = jnp.zeros((tile, rows), jnp.bfloat16)
            for m in range(per_owner):
                found = jnp.where(here == ids[m : m + 1, :], marks[m : m + 1, :], found)
            marks_all[slot, pl.ds(first, tile), lanes] = found
            return carry

        lax.fori_loop(0, reps * tiles, step, 0)

    def score(slot, buffer):
        score_ref[...] = (
            dot_nt(docs_all[slot], unit_all[...].reshape(all_rows, width)) * score_scale
        )
        for at in range(reps):
            lanes = pl.ds(at * rows, rows)

            def step(index, totals):
                span = pl.ds(pl.multiple_of(index * tile, tile), tile)
                marks = marks_all[slot, span, lanes].astype(jnp.float32)
                scores = score_ref[span, lanes]
                held = marks > 0.5
                raised = jnp.where(held, jnp.exp(scores), 0.0)
                target = jnp.where(held, jnp.exp(marks - 1.0), 0.0) * label_sum[at, 0:1, :]
                weight_ref[buffer, 0, span, lanes] = raised.astype(jnp.bfloat16)
                weight_ref[buffer, 1, span, lanes] = (target * pull_scale).astype(jnp.bfloat16)
                return (
                    totals[0] + jnp.sum(raised, axis=0, keepdims=True),
                    totals[1] + jnp.sum(target * scores, axis=0, keepdims=True),
                    totals[2] + jnp.sum(raised * scores, axis=0, keepdims=True),
                )

            zero = jnp.zeros((1, rows), jnp.float32)
            norm, dotted, spread = lax.fori_loop(0, tiles, step, (zero, zero, zero))
            stats[at, 0:1, :] += norm
            stats[at, 1:2, :] += dotted
            stats[at, 2:3, :] += spread

    def accumulate(slots, first):
        for kind in range(2):
            turned = [weight_ref[buffer, kind].T for buffer in range(len(slots))]
            for at in range(reps):
                terms = [
                    jnp.dot(
                        part,
                        docs_all[slot, :, at * block : (at + 1) * block],
                        preferred_element_type=jnp.float32,
                    )
                    for part, slot in zip(turned, slots)
                ]
                if first:
                    sums[at, kind] = sum(terms)
                else:
                    sums[at, kind] += sum(terms)

    def between(index, way):
        if index == 0 and way == 0:
            for copy in meta_copies:
                copy.wait_recv()
            for at in range(reps):
                raised_labels = jnp.exp(
                    meta_all[at, candidates : 2 * candidates, :].astype(jnp.float32)
                )
                label_sum[at, 0:1, :] = 1.0 / jnp.sum(raised_labels, axis=0, keepdims=True)
        if index < 2:
            share = groups // 4
            first = (2 * index + way) * share
            for slot in range(first, first + share):
                label_mask(slot)
        elif index == 2 and way == 0:
            for copy in unit_copies:
                copy.wait_recv()
            for copy in raw_copies + radius_copies:
                copy.start()
            score(0, 0)
            accumulate((0,), True)
        elif index == 2:
            score(1, 0)
        elif index == 3 and way == 0:
            score(groups - 1, 1)
            accumulate((1, groups - 1), False)
        elif index % 2 == 0 and way == 0 and index < ring_steps - 1:
            score(index // 2, 0)
        elif index % 2 == 0 and index < ring_steps - 1:
            score(groups - index // 2, 1)
            accumulate((index // 2, groups - index // 2), False)
        elif index == ring_steps - 2 and way == 0:
            score(groups // 2 - 1, 0)
        elif index == ring_steps - 2:
            score(groups // 2 + 1, 1)
            accumulate((groups // 2 - 1, groups // 2 + 1), False)
            for copy in raw_copies:
                copy.wait_recv()
            for at in range(reps):
                raw_turned[:, at * rows : (at + 1) * rows] = raw_all[at].T

    for index in range(ring_steps):
        for way in range(2):
            ring_copy(way, index).wait_recv()
            if index + 2 < ring_steps:
                ring_copy(way, index + 2).start()
            between(index, way)
    score(groups // 2, 0)
    stat_copies = rep_copies(4, lambda at: stats, lambda at: stats_in.at[at])
    for copy in stat_copies:
        copy.start()
    last_turned = [weight_ref[0, kind].T for kind in range(2)]

    def accumulate_last(at):
        span = pl.ds(pl.multiple_of(at * block, block), block)
        for kind in range(2):
            sums[at, kind] += jnp.dot(
                last_turned[kind], docs_all[groups // 2, :, span], preferred_element_type=jnp.float32
            )

    accumulate_last(pair_cross)

    def pull_copy(at, source, landing, peer):
        return pltpu.make_async_remote_copy(
            src_ref=source,
            dst_ref=landing,
            send_sem=pull_send.at[at],
            recv_sem=pull_recv.at[at],
            device_id=(docs_at, peer),
            device_id_type=MESH,
        )

    pair_out[...] = sums[pair_cross].astype(jnp.bfloat16)
    pair_copy = pull_copy(0, pair_out, pair_in, pair)
    pair_copy.start()
    for at in (cross, pair, rep_at):
        accumulate_last(at)
    for copy in stat_copies:
        copy.wait_recv()
    shares, projections = [], []
    for at in range(reps):
        total = stats[at]
        for origin in range(others):
            total = total + stats_in[origin, at]
        stats_in[0, at] = total
        shares.append((pull_scale / total).T[:, 0:1])
        projected = (total[2:3, :] / total[0:1, :] - total[1:2, :]) * (LOSS_SCALE / width)
        projections.append(jnp.broadcast_to(projected, total.shape).T[:, 0:1])
    own_stats = stats_in[0, rep_at]
    loss_ref[...] = jnp.log(own_stats[0:1, :]) - own_stats[1:2, :]
    pair_copy.wait_recv()
    cross_copies = []
    for at in range(reps):
        span = pl.ds(at * rows, rows)
        raised = sums[cross, 0, span, :] + pair_in[0, span, :].astype(jnp.float32)
        target = sums[cross, 1, span, :] + pair_in[1, span, :].astype(jnp.float32)
        cross_out[at] = (raised * shares[at] - target).astype(jnp.bfloat16)
        copy = pull_copy(2 + at, cross_out.at[at], cross_in.at[at], cross)
        copy.start()
        cross_copies.append(copy)
    for at in range(reps):
        span = pl.ds(at * rows, rows)
        near_out[at] = (sums[pair, 0, span, :] * shares[at] - sums[pair, 1, span, :]).astype(
            jnp.bfloat16
        )
    near_copy = pull_copy(1, near_out, near_in, pair)
    near_copy.start()
    for at in range(reps):
        span = pl.ds(at * rows, rows)
        pull_ref[at] = sums[rep_at, 0, span, :] * shares[at] - sums[rep_at, 1, span, :]
    near_copy.wait_recv()
    for copy in radius_copies:
        copy.wait_recv()
    own_cols = pl.ds(pl.multiple_of(rep_at * block, block), block)
    group_terms = None
    for at in range(reps):
        held = pull_ref[at] + near_in[at].astype(jnp.float32)
        unit = unit_all[at, :, own_cols].astype(jnp.float32)
        cross_copies[at].wait_recv()
        held = held + cross_in[at].astype(jnp.float32)
        grad_cols[at] = ((held - unit * projections[at]) / radius_all[at, :, 0:1]).astype(
            jnp.bfloat16
        )
        if at == reps // 2 - 1:
            group_terms = jnp.dot(
                raw_turned[:, 0 : all_rows // 2],
                grad_cols[0 : reps // 2].reshape(all_rows // 2, block),
                preferred_element_type=jnp.float32,
            )
    grad_copies = rep_copies(5, lambda peer: grad_cols.at[peer], own_block(grad_home))
    for copy in grad_copies:
        copy.start()
    out_rows = width // groups
    parts = 2
    piece = block // parts
    group_terms += jnp.dot(
        raw_turned[:, all_rows // 2 :],
        grad_cols[reps // 2 :].reshape(all_rows // 2, block),
        preferred_element_type=jnp.float32,
    )
    group_terms = group_terms.astype(jnp.bfloat16).reshape(groups, out_rows, block)
    for part in range(parts):
        terms_out[part] = group_terms[:, :, part * piece : (part + 1) * piece]
    far_first = sorted(range(1, groups), key=lambda step: abs(step - groups // 2))
    term_copies = []
    for part in range(parts):
        for step in far_first:
            peer = lax.rem(docs_at + step, groups)
            copy = pltpu.make_async_remote_copy(
                src_ref=terms_out.at[part, peer],
                dst_ref=terms_in.at[part, step - 1],
                send_sem=terms_send.at[part, step - 1],
                recv_sem=terms_recv.at[part, step - 1],
                device_id=(peer, rep_at),
                device_id_type=MESH,
            )
            copy.start()
            term_copies.append(copy)
    grad_home[rep_at] = grad_cols[rep_at]
    for copy in grad_copies:
        copy.wait_recv()
    query_grad = dot_nt(grad_home[0], adapter_ref[:, 0:block])
    for at in range(1, reps):
        query_grad += dot_nt(grad_home[at], adapter_ref[:, at * block : (at + 1) * block])
    query_grad_ref[...] = query_grad.astype(jnp.bfloat16)
    final_copies = []
    for part in range(parts):
        summed = terms_out[part, docs_at].astype(jnp.float32)
        for at in range(groups - 1):
            term_copies[part * (groups - 1) + at].wait_recv()
        for at in range(groups - 1):
            summed = summed + terms_in[part, at].astype(jnp.float32)
        final_cols[part, rep_at] = (summed * inverse_root).astype(jnp.bfloat16)
        for at in range(others):
            copy = pltpu.make_async_remote_copy(
                src_ref=final_cols.at[part, rep_at],
                dst_ref=final_cols.at[part, rep_at],
                send_sem=final_send.at[part, at],
                recv_sem=final_recv.at[part, at],
                device_id=(docs_at, rep_peer(at + 1)),
                device_id_type=MESH,
            )
            copy.start()
            final_copies.append(copy)
    for part in range(parts):
        for at in range(others):
            final_copies[part * others + at].wait_recv()
        for at in range(reps):
            low = at * block + part * piece
            adapter_grad_ref[:, low : low + piece] = final_cols[part, at]

    for index in range(ring_steps):
        for way in range(2):
            ring_copy(way, index).wait_send()
    for copy in (
        meta_copies + unit_copies + radius_copies + raw_copies + stat_copies
        + [pair_copy, near_copy] + cross_copies + grad_copies
        + term_copies + final_copies
    ):
        copy.wait_send()


def gathered_on_device(queries, adapter, doc_table, routes, doc_rows, labels):
    groups = lax.axis_size("docs")
    reps = lax.axis_size("rep")
    rows, width = queries.shape
    fanout = routes.shape[1]
    per_owner = doc_rows.shape[2]
    doc_count = doc_table.shape[0]
    candidates = fanout * per_owner
    block = width // reps
    out_rows = width // groups
    others = reps - 1
    all_rows = reps * rows
    meta = jnp.concatenate(
        [
            doc_rows.reshape(rows, candidates),
            labels.reshape(rows, candidates),
            routes,
            jnp.zeros((rows, 16 - fanout), jnp.int32),
        ],
        axis=1,
    ).T
    bf16, f32 = jnp.bfloat16, jnp.float32
    vmem = pltpu.VMEM
    dma = pltpu.SemaphoreType.DMA
    losses, query_grads, adapter_grad = pl.pallas_call(
        functools.partial(
            gathered_kernel, groups, reps, fanout, per_owner,
            1.0 / math.sqrt(rows * groups * reps),
        ),
        out_shape=(
            jax.ShapeDtypeStruct((1, rows), f32),
            jax.ShapeDtypeStruct((rows, width), bf16),
            jax.ShapeDtypeStruct((out_rows, width), bf16),
        ),
        in_specs=[pl.BlockSpec(memory_space=pl.ANY)] * 4,
        out_specs=[pl.BlockSpec(memory_space=vmem)] * 3,
        scratch_shapes=[
            vmem((width, width), bf16),
            vmem((doc_count, width), bf16),
            vmem((groups, doc_count, width), bf16),
            vmem((reps, rows, width), bf16),
            vmem((reps, rows, width), bf16),
            vmem((2 * candidates + 16, rows), jnp.int32),
            vmem((reps, 2 * candidates + 16, rows), bf16),
            vmem((reps, rows, 128), f32),
            vmem((groups, doc_count, all_rows), bf16),
            vmem((doc_count, rows), bf16),
            vmem((width, all_rows), bf16),
            vmem((doc_count, all_rows), f32),
            vmem((2, 2, doc_count, all_rows), bf16),
            vmem((reps, 2, all_rows, block), f32),
            vmem((reps, 8, rows), f32),
            vmem((reps, 8, rows), f32),
            vmem((others, reps, 8, rows), f32),
            vmem((2, all_rows, block), bf16),
            vmem((2, all_rows, block), bf16),
            vmem((reps, rows, block), bf16),
            vmem((reps, rows, block), bf16),
            vmem((reps, rows, block), bf16),
            vmem((reps, rows, block), bf16),
            vmem((reps, rows, block), f32),
            vmem((reps, rows, block), bf16),
            vmem((reps, rows, block), bf16),
            vmem((2, groups, out_rows, block // 2), bf16),
            vmem((2, groups - 1, out_rows, block // 2), bf16),
            vmem((2, reps, out_rows, block // 2), bf16),
            dma((4,)),
            dma((2, groups - 1)),
            dma((2, groups - 1)),
            dma((6, others)),
            dma((6, others)),
            dma((2 + reps,)),
            dma((2 + reps,)),
            dma((2, groups - 1)),
            dma((2, groups - 1)),
            dma((2, others)),
            dma((2, others)),
        ],
        compiler_params=pltpu.CompilerParams(
            collective_id=0, has_side_effects=True, vmem_limit_bytes=213 * 256 * 1024
        ),
    )(
        queries, adapter, doc_table, meta,
    )
    return (losses.reshape(rows), query_grads, adapter_grad)


def on_device(queries, adapter, doc_table, routes, doc_rows, labels):
    gathered_bytes = lax.axis_size("docs") * doc_table.size * doc_table.dtype.itemsize
    if gathered_bytes <= GATHER_LIMIT and lax.axis_size("rep") == 4:
        return gathered_on_device(queries, adapter, doc_table, routes, doc_rows, labels)
    return routed_on_device(queries, adapter, doc_table, routes, doc_rows, labels)


def solution(mesh):
    placed = (
        P(("docs", "rep"), None),
        P(),
        P(("docs", "rep"), None),
        P(("docs", "rep"), None),
        P(("docs", "rep"), None, None),
        P(("docs", "rep"), None, None),
    )
    return jax.shard_map(
        on_device,
        mesh=mesh,
        in_specs=placed,
        out_specs=(P(("docs", "rep")), P(("docs", "rep"), None), P("docs", None)),
        check_vma=False,
    )
```
